1024 devices in a mesh: dp: 4 (over z_hi), expert: 8 (over y), tensor: 32 (over x, z_lo, core).
Axes of the slice: x: 4, y: 8, z: 16 (z_hi: 4, z_lo: 4; z = z_hi * 4 + z_lo), core: 2. Of those that a mesh axis runs over, the one named last changes fastest.
Arguments:
- tokens: bfloat16 [4096, 7168], P(('dp', 'expert'), 'tensor'), may hold values from -6 to 6
- cotangent: bfloat16 [4096, 7168], P(('dp', 'expert'), 'tensor'), may hold values from -6 to 6
- route_ids: int32 [4096, 8], P(('dp', 'expert')), may hold values from 0 to 255, all different within a row; in each aligned block of 128 rows (0 to 127, 128 to 255, ...) at most 7 rows name the same one
- gates: float32 [4096, 8], P(('dp', 'expert')), may hold values from 0.2 to 1.2
- w_gate: bfloat16 [16384, 7168], P(('expert', 'tensor')), may hold values from -0.0625 to 0.0625
- w_up: bfloat16 [16384, 7168], P(('expert', 'tensor')), may hold values from -0.0625 to 0.0625
- w_down: bfloat16 [16384, 7168], P(('expert', 'tensor')), may hold values from -0.125 to 0.125
Outputs:
- mixed: bfloat16 [4096, 7168], P(('dp', 'expert'), 'tensor')
- token_grad: bfloat16 [4096, 7168], P(('dp', 'expert'), 'tensor')
- gate_grad: bfloat16 [16384, 7168], P(('expert', 'tensor'), 'dp')
- up_grad: bfloat16 [16384, 7168], P(('expert', 'tensor'), 'dp')
- down_grad: bfloat16 [16384, 7168], P(('expert', 'tensor'), 'dp')
The draws below stay inside these ranges and needn't reach their ends.
Inputs may be any that keep to these rules, and one draw needn't show every extreme that they name: `route_ids`: each token names 8 different experts. Among the 128 tokens of one block, no expert is named by more than 7 tokens.
All inputs are finite; a program needn't handle non-finite values.
Results may differ from the reference program's by a relative error of at most 0.034.
Values may be sent and summed in bfloat16 or wider, within the bound.
A program may use at most 64 MiB of HBM per device.

```python
import math
import jax
import jax.numpy as jnp
import numpy as np
from jax import lax

D = 7168
FF = 2048
EXPERTS = 256
TOP = 8
TOK_DEV = 128
CAP = 7
EXP_WIN = 8
HID_DEV = 64
TOKENS = 4096
N_DP = 4


def steps_of(rng, extent, cuts, smallest, high):
    loudness, own = 1.0, jax.random.fold_in(rng, 6)
    for axis_at, blocks in cuts:
        draws = jnp.exp(jax.random.uniform(jax.random.fold_in(own, axis_at), (blocks,), jnp.float32, smallest / len(cuts), high / len(cuts)))
        loudness = loudness * jnp.repeat(draws, extent[axis_at] // blocks).reshape([-1 if axis == axis_at else 1 for axis in range(len(extent))])
    return loudness


def routed_block(own_key, own, number, rows, number_of, top, limit, skew):
    order = jax.random.permutation(own_key, number_of)
    packed, common = shares(number_of, rows * top, limit, skew, True), shares(number_of, rows * top, limit, skew, False)
    places = jnp.arange(number_of)

    def named(lengths, rotation):
        used = int((lengths > 0).sum())
        fixed = max(1, used // 4)
        passed = fixed + (places - fixed + rotation * (used - fixed)) % max(1, number_of - fixed)
        return jnp.zeros((number_of,), jnp.int32).at[order[jnp.where(places < fixed, places, passed)]].set(jnp.asarray(lengths, jnp.int32))

    lengths = jnp.where(number % 4 == 0, named(packed, number // 4), named(common, number - number // 4 - 1))
    mixed = jax.random.permutation(jax.random.fold_in(own, 3), number_of)
    giver, sink = mixed[0:number_of // 2 * 2:2], mixed[1:number_of // 2 * 2:2]
    slack = jnp.minimum(lengths[giver] - 1, limit - lengths[sink]) // 2
    slack = jnp.where((giver == order[0]) | (sink == order[0]) | (lengths[sink] == 0), 0, jnp.maximum(slack, 0))
    passed = jax.random.randint(jax.random.fold_in(own, 4), (number_of // 2,), 0, 1 << 20) % (slack + 1)
    lengths = lengths.at[giver].add(-passed).at[sink].add(passed)
    members = jnp.searchsorted(jnp.cumsum(lengths), jnp.arange(rows * top), side="right").astype(jnp.int32)
    grid = members.reshape(top, rows).T
    grid = grid[jax.random.permutation(jax.random.fold_in(own, 1), rows)]
    rotation = jax.random.randint(jax.random.fold_in(own, 2), (rows, 1), 0, top)
    return jnp.take_along_axis(grid, (jnp.arange(top)[None, :] + rotation) % top, axis=1)


def shares(number_of, total, bound, slope, full):
    portions = [(1 << 20) // math.isqrt(standing ** slope) + 1 for standing in range(1, number_of + 1)]
    largest = bound if full else min(bound, max(-(-total // number_of), total * portions[0] // sum(portions)))
    least = 1 if total - largest >= number_of - 1 else 0
    holding, rest = [largest] + [least] * (number_of - 1), total - largest - least * (number_of - 1)
    while rest > 0:
        free = [i for i in range(1, number_of) if holding[i] < largest] or [i for i in range(1, number_of) if holding[i] < bound]
        whole, budget = sum([portions[i] for i in free]), rest
        for i in free:
            addition = min(bound - holding[i], max(1, budget * portions[i] // whole), rest)
            holding[i] = holding[i] + addition
            rest = rest - addition
    return np.array(holding)


def centred(key, extent, deviation, most, cuts=(), kind=jnp.bfloat16):
    array = deviation * jax.random.normal(key, extent, jnp.float32)
    if cuts:
        array = array * steps_of(key, extent, cuts, -0.22, 0.18)
    return jnp.clip(array, -most, most).astype(kind)


def setup_inputs(seed: int = 0) -> dict:
    arg_keys = jax.random.split(jax.random.key(seed), 8)
    tokens = centred(arg_keys[0], (TOKENS, D), 1.0, 6.0, ((0, 32), (1, 32)))
    cotangent = centred(arg_keys[1], (TOKENS, D), 1.0, 6.0, ((0, 32), (1, 32)))
    route_ids_keys = jax.random.split(jax.random.fold_in(arg_keys[2], 1), TOKENS // TOK_DEV)
    route_ids_turns = jax.random.permutation(jax.random.fold_in(arg_keys[2], 3), TOKENS // TOK_DEV)
    route_ids = jax.vmap(lambda own, number: routed_block(jax.random.fold_in(arg_keys[2], 2), own, number, TOK_DEV, EXPERTS, TOP, CAP, 2))(route_ids_keys, route_ids_turns).reshape((TOKENS, TOP))
    gates = jnp.clip(0.2 + 1 * jax.random.uniform(arg_keys[3], (TOKENS, TOP), jnp.float32) ** steps_of(arg_keys[3], (TOKENS, TOP), ((0, 32),), -0.2, 0.2), 0.2, 1.2)
    w_gate = centred(arg_keys[4], (EXP_WIN * FF, D), D ** -0.5, 0.0625, ((0, 256),))
    w_up = centred(arg_keys[5], (EXP_WIN * FF, D), D ** -0.5, 0.0625, ((0, 256),))
    w_down = centred(arg_keys[6], (EXP_WIN * FF, D), FF ** -0.5, 0.125, ((0, 256),))
    return dict(tokens=tokens, cotangent=cotangent, route_ids=route_ids, gates=gates, w_gate=w_gate, w_up=w_up, w_down=w_down)


def blockwise(pairs, rows):
    pieces = FF // HID_DEV
    total = None
    for left, right in pairs:
        lp = left.reshape(rows, pieces, HID_DEV).astype(jnp.float32)
        rp = right.reshape(pieces, HID_DEV, D).astype(jnp.float32)
        term = jnp.einsum('rph,phd->prd', lp, rp)
        total = term if total is None else total + term
    rounded = total.astype(jnp.bfloat16)
    return lax.optimization_barrier(jnp.sum(rounded.astype(jnp.float32), axis=0)).astype(jnp.bfloat16)

def group_grad(left, right, group_rows):
    lg = left.reshape(N_DP, group_rows, D).astype(jnp.float32)
    rg = right.reshape(N_DP, group_rows, FF).astype(jnp.float32)
    total = jnp.zeros((FF, D), jnp.float32)
    for group in range(N_DP):
        part = jnp.dot(rg[group].T, lg[group]).astype(jnp.bfloat16)
        total = total + part.astype(jnp.float32)
    return total.astype(jnp.bfloat16)

def reference(tokens, cotangent, route_ids, gates, w_gate, w_up, w_down):
    blocks = TOKENS // TOK_DEV
    rows = blocks * CAP
    group_rows = rows // N_DP
    tok_blocks = tokens.reshape(blocks, TOK_DEV, D).astype(jnp.float32)
    cot_blocks = cotangent.reshape(blocks, TOK_DEV, D).astype(jnp.float32)
    slot_iota = jnp.arange(CAP, dtype=jnp.int32)

    def per_expert(carry, expert):
        out_acc, grad_acc = carry
        match = route_ids == expert
        hits = lax.optimization_barrier(jnp.sum(match.astype(jnp.int32), axis=1)).reshape(blocks, TOK_DEV)
        weight_of = lax.optimization_barrier(jnp.sum(jnp.where(match, gates, jnp.zeros_like(gates)), axis=1)).reshape(blocks, TOK_DEV)
        places = jnp.cumsum(hits, axis=1) - 1
        picks = ((hits[:, None, :] == 1) & (places[:, None, :] == slot_iota[None, :, None])).astype(jnp.float32)
        slot_rows = jnp.einsum('bct,btd->bcd', picks, tok_blocks).astype(jnp.bfloat16).reshape(rows, D)
        cot_rows = jnp.einsum('bct,btd->bcd', picks, cot_blocks)
        slot_gate = jnp.einsum('bct,bt->bc', picks, weight_of)
        scaled = (slot_gate[:, :, None] * cot_rows).astype(jnp.bfloat16).reshape(rows, D)
        start = (expert * FF).astype(jnp.int32)
        wg = lax.dynamic_slice_in_dim(w_gate, start, FF, 0)
        wu = lax.dynamic_slice_in_dim(w_up, start, FF, 0)
        wd = lax.dynamic_slice_in_dim(w_down, start, FF, 0)
        pre = jnp.dot(slot_rows, wg.T, preferred_element_type=jnp.float32)
        upper = jnp.dot(slot_rows, wu.T, preferred_element_type=jnp.float32)
        sig = jax.nn.sigmoid(pre)
        act = pre * sig
        hidden = (act * upper).astype(jnp.bfloat16)
        expert_out = blockwise([(hidden, wd)], rows)
        back = jnp.dot(scaled, wd.T, preferred_element_type=jnp.float32)
        gate_delta = (back * upper * sig * (1.0 + pre * (1.0 - sig))).astype(jnp.bfloat16)
        up_delta = (back * act).astype(jnp.bfloat16)
        input_delta = blockwise([(gate_delta, wg), (up_delta, wu)], rows)
        gate_part = group_grad(slot_rows, gate_delta, group_rows)
        up_part = group_grad(slot_rows, up_delta, group_rows)
        down_part = group_grad(scaled, hidden, group_rows)
        out_add = jnp.einsum('bct,bcd->btd', picks, expert_out.reshape(blocks, CAP, D).astype(jnp.float32))
        out_add = out_add * weight_of[:, :, None]
        grad_add = jnp.einsum('bct,bcd->btd', picks, input_delta.reshape(blocks, CAP, D).astype(jnp.float32))
        out_acc = out_acc + out_add.reshape(TOKENS, D)
        grad_acc = grad_acc + grad_add.reshape(TOKENS, D)
        return ((out_acc, grad_acc), (gate_part, up_part, down_part))
    start_carry = (jnp.zeros((TOKENS, D), jnp.float32), jnp.zeros((TOKENS, D), jnp.float32))
    (out_acc, grad_acc), stacked = lax.scan(per_expert, start_carry, jnp.arange(EXP_WIN, dtype=jnp.int32))

    def spread(stack):
        return stack.reshape(EXP_WIN * FF, D)
    return (out_acc.astype(jnp.bfloat16), grad_acc.astype(jnp.bfloat16), spread(stacked[0]), spread(stacked[1]), spread(stacked[2]))
```

```python
import jax
import jax.numpy as jnp
from jax import lax
from jax.experimental import pallas as pl
from jax.experimental.pallas import tpu as pltpu
from jax.sharding import PartitionSpec as P

NX, NZ, NC = 4, 4, 2
NY = 8
NDP = 4
CHUNKS = NX * NZ * NC
BLK = 16
ROWS = NY * BLK
HALF = ROWS // 2
QUART = ROWS // 4
LANES = 256
HID = 64
N_SEMS = 208
BF16 = jnp.bfloat16
F32 = jnp.float32


def wrap(value, size):
    return lax.rem(value, size)


def nt_dot(left, right):
    return lax.dot_general(left, right, (((1,), (1,)), ((), ())), preferred_element_type=F32)


def kernel(
    tok, cot, rid, gat, wg, wu, wd,
    mixed, tgrad, ggrad, ugrad, dgrad,
    wraw, wt, disp, chunk, acc, mine, compact,
    extra, part, kept, sib_in, opp_out, opp_a, opp_b, right_out, left_out,
    from_left, from_right, z_out, z_in, total, ret_out, ret, gbuf, sems,
):
    dp = lax.axis_index("dp")
    y = lax.axis_index("expert")
    t = lax.axis_index("tensor")
    x = t // (NZ * NC)
    z = wrap(t // NC, NZ)
    c = wrap(t, NC)
    other = 1 - c
    xr, xl, xo = wrap(x + 1, NX), wrap(x + 3, NX), wrap(x + 2, NX)
    cols = tok.shape[1]
    count = [0]

    def take(n=1):
        base = count[0]
        count[0] += n
        assert count[0] <= N_SEMS
        return base

    def tensor_at(x_, z_, c_):
        return {"tensor": x_ * (NZ * NC) + z_ * NC + c_}

    def at(c_, x_, z_):
        return c_ * (NX * NZ) + x_ * NZ + z_

    sibling = tensor_at(x, z, other)
    right, left = tensor_at(xr, z, c), tensor_at(xl, z, c)

    def z_peer(k):
        return tensor_at(x, wrap(z + k, NZ), c)

    def y_peer(k):
        return {"expert": wrap(y + k, NY)}

    def dp_peer(k):
        return {"dp": wrap(dp + k, NDP)}

    barrier = pltpu.get_barrier_semaphore()
    partners = [y_peer(k) for k in range(1, NY)]
    partners += [z_peer(k) for k in range(1, NZ)]
    partners += [dp_peer(k) for k in range(1, NDP)]
    partners += [sibling, right, left]
    for where in partners:
        pl.semaphore_signal(barrier, inc=1, device_id=where, device_id_type=pl.DeviceIdType.MESH)

    def send(src, dst, recv, where):
        copy = pltpu.make_async_remote_copy(
            src_ref=src, dst_ref=dst, send_sem=sems.at[take()], recv_sem=sems.at[recv],
            device_id=where, device_id_type=pl.DeviceIdType.MESH,
        )
        copy.start()
        return copy

    def arrived(ref, sem):
        pltpu.make_async_copy(ref, ref, sems.at[sem]).wait()

    loads = []
    for i, ref in enumerate((wg, wu, wd)):
        copy = pltpu.make_async_copy(ref, wraw.at[i], sems.at[take()])
        copy.start()
        loads.append(copy)

    lane = lax.broadcasted_iota(jnp.int32, (ROWS, ROWS), 1)
    row = lax.broadcasted_iota(jnp.int32, (ROWS, ROWS), 0)
    label = lane // BLK
    routes, weights = rid[...], gat[...]
    hits = jnp.zeros((ROWS, ROWS), F32)
    weight_of = jnp.zeros((ROWS, ROWS), F32)
    for k in range(routes.shape[1]):
        same = routes[:, k : k + 1] == label
        hits = hits + jnp.where(same, 1.0, 0.0)
        weight_of = weight_of + jnp.where(same, weights[:, k : k + 1], 0.0)
    lower = jnp.where(lane <= row, 1.0, 0.0).astype(BF16)
    places = jnp.dot(lower, hits.astype(BF16), preferred_element_type=F32) - 1.0
    slot = wrap(lane, BLK // 2).astype(F32)
    pick = jnp.where((hits == 1.0) & (places == slot), 1.0, 0.0)
    first_lane = wrap(lane // (BLK // 2), 2) == 0
    first_row = wrap(row // (BLK // 2), 2) == 0
    pick_t = jnp.transpose(pick)
    slot_gate = jnp.sum(jnp.transpose(pick * weight_of), axis=1, keepdims=True)
    pick_tok = jnp.where(first_row, pick_t, 0.0).astype(BF16)
    pick_cot = jnp.where(first_row, 0.0, pick_t).astype(BF16)
    rows_tok = jnp.dot(pick_tok, tok[...], preferred_element_type=F32)
    rows_cot = jnp.dot(pick_cot, cot[...], preferred_element_type=F32)
    disp[...] = jnp.zeros_like(disp)
    disp[:, 0:cols] = (rows_tok + slot_gate * rows_cot).astype(BF16)

    pl.semaphore_wait(barrier, len(partners))

    me = at(c, x, z)
    my_rows = pl.ds(pl.multiple_of(y * BLK, BLK), BLK)
    sent_y = []
    y_in = take(NY - 1)
    for k in range(1, NY):
        there = pl.ds(pl.multiple_of(wrap(y + k, NY) * BLK, BLK), BLK)
        sent_y.append(send(disp.at[there], chunk.at[me, my_rows], y_in + k - 1, y_peer(k)))
    chunk[me, my_rows, :] = disp[my_rows, :]

    for copy in loads:
        copy.wait()
    wt[:, :, LANES // 2 :] = jnp.zeros((CHUNKS, LANES, LANES // 2), BF16)
    wt[:, 3 * HID :, : LANES // 2] = jnp.zeros((CHUNKS, LANES - 3 * HID, LANES // 2), BF16)
    for tt in range(CHUNKS):
        g = at(tt % NC, tt // (NZ * NC), (tt // NC) % NZ)
        for i in range(3):
            wt[g, HID * i : HID * (i + 1), 0:cols] = wraw[i, :, cols * tt : cols * (tt + 1)]
    acc[...] = jnp.zeros_like(acc)

    for k in range(1, NY):
        from_y = pl.ds(pl.multiple_of(wrap(y + NY - k, NY) * BLK, BLK), BLK)
        arrived(chunk.at[me, from_y], y_in + k - 1)

    def consume(g):
        acc[...] += nt_dot(chunk[g], wt[g])

    sib_sem = take(NX * NZ)
    z_sem = take(NZ - 1)
    left_sem, right_sem = take(NZ), take(NZ)
    oa_sem, ob_sem = take(NZ), take(NZ)
    sent_g = []

    def to_sibling(x_, z_):
        g = at(c, x_, z_)
        sent_g.append(send(chunk.at[g], chunk.at[g], sib_sem + x_ * NZ + z_, sibling))

    def z_at(k):
        return wrap(z + NZ - k, NZ)

    for k in range(NZ):
        zk = z_at(k)
        g = at(c, x, zk)
        if k > 0:
            arrived(chunk.at[g], z_sem + k - 1)
        sent_g.append(send(chunk.at[g], chunk.at[g], left_sem + zk, right))
        sent_g.append(send(chunk.at[g], chunk.at[g], right_sem + zk, left))
        if k == 0:
            for j in range(1, NZ):
                sent_g.append(send(chunk.at[g], chunk.at[g], z_sem + j - 1, z_peer(j)))
        to_sibling(x, zk)
        consume(g)
    for k in range(NZ):
        zk = z_at(k)
        g = at(c, xl, zk)
        half = (g, pl.ds(0, HALF))
        arrived(chunk.at[g], left_sem + zk)
        sent_g.append(send(chunk.at[half], chunk.at[half], oa_sem + zk, right))
        to_sibling(xl, zk)
        consume(g)
        g = at(c, xr, zk)
        half = (g, pl.ds(HALF, HALF))
        arrived(chunk.at[g], right_sem + zk)
        sent_g.append(send(chunk.at[half], chunk.at[half], ob_sem + zk, left))
        to_sibling(xr, zk)
        consume(g)
    for k in range(NZ):
        zk = z_at(k)
        g = at(c, xo, zk)
        arrived(chunk.at[g, pl.ds(0, HALF)], oa_sem + zk)
        arrived(chunk.at[g, pl.ds(HALF, HALF)], ob_sem + zk)
        to_sibling(xo, zk)
        consume(g)

    quarter = pl.ds(pl.multiple_of(x * QUART, QUART), QUART)
    q_sem = take(NDP - 1)
    sent_q = []
    for k in range(1, NDP):
        src = chunk.at[at(c, wrap(dp + k, NDP), z), quarter]
        sent_q.append(send(src, extra.at[k - 1, c * NZ + z, quarter], q_sem + k - 1, dp_peer(k)))

    for x_ in (x, xl, xr, xo):
        for k in range(NZ):
            zk = z_at(k)
            g = at(other, x_, zk)
            arrived(chunk.at[g], sib_sem + x_ * NZ + zk)
            consume(g)

    whole = acc[...].reshape(NY, 2, BLK // 2, LANES)
    half_rows = NY * BLK // 2
    fwd = whole[:, 0].reshape(half_rows, LANES)[:, : 2 * HID]
    bwd = whole[:, 1].reshape(half_rows, LANES)[:, 2 * HID :]
    low = lax.broadcasted_iota(jnp.int32, (half_rows, 2 * HID), 1) < HID
    turned = pltpu.roll(fwd, HID, 1)
    pre = jnp.where(low, fwd, turned)
    upper = jnp.where(low, turned, fwd)
    back = bwd + pltpu.roll(bwd, HID, 1)
    sig = jax.nn.sigmoid(pre)
    act = pre * sig
    hidden = act * upper
    gate_delta = back * upper * sig * (1.0 + pre * (1.0 - sig))
    up_delta = back * act
    deltas = jnp.where(low, gate_delta, up_delta)
    hid = jnp.where(low, hidden, 0.0)
    compact[NDP - 1] = jnp.concatenate([deltas, hid], axis=1).astype(BF16)
    zeros = jnp.zeros((NY, BLK // 2, 2 * HID), F32)
    top = jnp.concatenate([zeros, hid.reshape(NY, BLK // 2, 2 * HID)], axis=2)
    bottom = jnp.concatenate([deltas.reshape(NY, BLK // 2, 2 * HID), zeros], axis=2)
    mine[...] = jnp.concatenate([top, bottom], axis=1).reshape(ROWS, LANES).astype(BF16)

    m_sem = take(NDP - 1)
    sent_m = []
    for k in range(1, NDP):
        sent_m.append(send(compact.at[NDP - 1], compact.at[k - 1], m_sem + k - 1, dp_peer(k)))

    sr_sem = take(NZ)
    xa_sem, xb_sem = take(NZ), take(NZ)
    nl_sem, nr_sem = take(NZ), take(NZ)
    zr_sem = take(NZ - 1)
    sent_r = []

    def stage_a(k):
        zk = wrap(z + k + 1, NZ)
        left_side = mine[...]

        def one(x_, carry):
            part[k, x_] = jnp.dot(
                left_side, wt[at(other, x_, zk)], preferred_element_type=F32
            ).astype(BF16)
            return carry

        lax.fori_loop(0, NX, one, 0)
        sent_r.append(send(part.at[k], sib_in.at[k], sr_sem + k, sibling))

        def two(x_, carry):
            kept[k, x_] = jnp.dot(left_side, wt[at(c, x_, zk)], preferred_element_type=F32)
            return carry

        lax.fori_loop(0, NX, two, 0)

    def pair(k, x_):
        return kept[k, x_] + sib_in[k, x_].astype(F32)

    def stage_b(k):
        arrived(sib_in.at[k], sr_sem + k)
        opp_out[k] = pair(k, xo).astype(BF16)
        sent_r.append(send(opp_out.at[k, pl.ds(0, HALF)], opp_a.at[k], xa_sem + k, right))
        sent_r.append(send(opp_out.at[k, pl.ds(HALF, HALF)], opp_b.at[k], xb_sem + k, left))

    def stage_c(k):
        arrived(opp_a.at[k], xa_sem + k)
        value = pair(k, xr)
        right_out[k, :HALF] = (value[:HALF] + opp_a[k].astype(F32)).astype(BF16)
        right_out[k, HALF:] = value[HALF:].astype(BF16)
        sent_r.append(send(right_out.at[k], from_left.at[k], nl_sem + k, right))
        arrived(opp_b.at[k], xb_sem + k)
        value = pair(k, xl)
        left_out[k, :HALF] = value[:HALF].astype(BF16)
        left_out[k, HALF:] = (value[HALF:] + opp_b[k].astype(F32)).astype(BF16)
        sent_r.append(send(left_out.at[k], from_right.at[k], nr_sem + k, left))

    def stage_d(k):
        arrived(from_left.at[k], nl_sem + k)
        arrived(from_right.at[k], nr_sem + k)
        value = pair(k, x) + from_left[k].astype(F32) + from_right[k].astype(F32)
        if k < NZ - 1:
            z_out[k] = value.astype(BF16)
            sent_r.append(send(z_out.at[k], z_in.at[k], zr_sem + k, z_peer(k + 1)))
        else:
            total[...] = value

    qz_sem = take(NZ - 1)
    ql_sem, qr_sem, qa_sem, qb_sem = take(), take(), take(), take()
    qs_sem = take()
    base = pl.multiple_of(c * NZ, NZ)
    strip = pl.ds(base, NZ)

    def part_rows(x_, start, size):
        return pl.ds(pl.multiple_of(x_ * QUART + start, BLK), size)

    def spread_1():
        for k in range(1, NDP):
            arrived(extra.at[k - 1, c * NZ + z, quarter], q_sem + k - 1)
        piece = extra.at[:, c * NZ + z, quarter]
        for k in range(1, NZ):
            sent_q.append(send(piece, piece, qz_sem + k - 1, z_peer(k)))

    def spread_2():
        for k in range(1, NZ):
            arrived(extra.at[:, c * NZ + z_at(k), quarter], qz_sem + k - 1)
        piece = extra.at[:, strip, quarter]
        sent_q.append(send(piece, piece, ql_sem, right))
        sent_q.append(send(piece, piece, qr_sem, left))

    def spread_3():
        arrived(extra.at[:, strip, part_rows(xl, 0, QUART)], ql_sem)
        piece = extra.at[:, strip, part_rows(xl, 0, QUART // 2)]
        sent_q.append(send(piece, piece, qa_sem, right))
        arrived(extra.at[:, strip, part_rows(xr, 0, QUART)], qr_sem)
        piece = extra.at[:, strip, part_rows(xr, QUART // 2, QUART // 2)]
        sent_q.append(send(piece, piece, qb_sem, left))

    def spread_4():
        arrived(extra.at[:, strip, part_rows(xo, 0, QUART // 2)], qa_sem)
        arrived(extra.at[:, strip, part_rows(xo, QUART // 2, QUART // 2)], qb_sem)
        piece = extra.at[:, strip]
        sent_q.append(send(piece, piece, qs_sem, sibling))

    stage_a(0)
    stage_a(1)
    stage_b(0)
    spread_1()
    stage_a(2)
    stage_b(1)
    stage_c(0)
    stage_a(3)
    stage_b(2)
    stage_c(1)
    spread_2()
    stage_d(0)
    stage_b(3)
    stage_c(2)
    stage_d(1)
    stage_c(3)
    spread_3()
    stage_d(2)
    stage_d(3)

    value = total[...]
    for k in range(NZ - 1):
        arrived(z_in.at[k], zr_sem + k)
        value = value + z_in[k].astype(F32)
    ret_out[...] = value.astype(BF16)

    yr_sem = take(NY - 1)
    for k in range(1, NY):
        there = pl.ds(pl.multiple_of(wrap(y + k, NY) * BLK, BLK), BLK)
        sent_r.append(send(ret_out.at[there], ret.at[my_rows], yr_sem + k - 1, y_peer(k)))
    ret[my_rows, :] = ret_out[my_rows, :]
    spread_4()

    for k in range(1, NDP):
        arrived(compact.at[k - 1], m_sem + k - 1)
    sides = []
    for k in range(NDP):
        both = compact[k].astype(F32).reshape(NY, BLK // 2, LANES)
        top = jnp.concatenate([both[:, :, : 2 * HID], zeros], axis=2)
        bottom = jnp.concatenate([zeros, both[:, :, 2 * HID :]], axis=2)
        side = jnp.concatenate([top, bottom], axis=1).reshape(ROWS, LANES)
        sides.append(jnp.transpose(side)[: 3 * HID].astype(BF16))
    gbuf[...] = jnp.zeros_like(gbuf)
    other_strip = pl.ds(pl.multiple_of(other * NZ, NZ), NZ)

    def gradient(c_, z_, offset):
        value = jnp.dot(sides[NDP - 1], chunk[at(c_, dp, z_)], preferred_element_type=F32)
        for k in range(1, NDP):
            value += jnp.dot(
                sides[k - 1], extra[k - 1, c_ * NZ + z_], preferred_element_type=F32
            )
        start = offset // 128 * 128
        shift = offset - start
        width = min(LANES + 128, gbuf.shape[1] - start)
        wide = value
        if width > LANES:
            wide = jnp.concatenate([value, jnp.zeros((3 * HID, width - LANES), F32)], axis=1)
        if shift:
            wide = pltpu.roll(wide, shift, 1)
        gbuf[:, start : start + width] += wide

    arrived(extra.at[:, other_strip], qs_sem)
    for z_ in range(NZ):
        for c_ in range(NC):
            gradient(c_, z_, cols * (z_ * NC + c_))
    ggrad[...] = gbuf[:HID].astype(BF16)
    ugrad[...] = gbuf[HID : 2 * HID].astype(BF16)
    dgrad[...] = gbuf[2 * HID :].astype(BF16)

    gates_hi = jnp.where(first_lane, pick * weight_of, 0.0)
    high = gates_hi.astype(BF16)
    low_part = (gates_hi - high.astype(F32)).astype(BF16)
    pick_ret = jnp.where(first_lane, 0.0, pick).astype(BF16)
    for k in range(1, NY):
        from_y = pl.ds(pl.multiple_of(wrap(y + NY - k, NY) * BLK, BLK), BLK)
        arrived(ret.at[from_y], yr_sem + k - 1)
    got = ret[...]
    out = jnp.dot(high, got, preferred_element_type=F32)
    out += jnp.dot(low_part, got, preferred_element_type=F32)
    mixed[...] = out[:, :cols].astype(BF16)
    tgrad[...] = jnp.dot(pick_ret, got, preferred_element_type=F32)[:, :cols].astype(BF16)

    for copy in sent_y + sent_g + sent_q + sent_m + sent_r:
        copy.wait_send()


def per_device(tokens, cotangent, route_ids, gates, w_gate, w_up, w_down):
    rows, cols = tokens.shape
    hid, width = w_gate.shape
    share = width // NDP
    vmem = pl.BlockSpec(memory_space=pltpu.VMEM)
    hbm = pl.BlockSpec(memory_space=pl.ANY)
    chunk_of = (ROWS, LANES)
    return pl.pallas_call(
        kernel,
        out_shape=(
            jax.ShapeDtypeStruct((rows, cols), BF16),
            jax.ShapeDtypeStruct((rows, cols), BF16),
            jax.ShapeDtypeStruct((hid, share), BF16),
            jax.ShapeDtypeStruct((hid, share), BF16),
            jax.ShapeDtypeStruct((hid, share), BF16),
        ),
        in_specs=[vmem] * 4 + [hbm] * 3,
        out_specs=[vmem] * 5,
        scratch_shapes=[
            pltpu.VMEM((3, hid, width), BF16),
            pltpu.VMEM((CHUNKS, LANES, LANES), BF16),
            pltpu.VMEM(chunk_of, BF16),
            pltpu.VMEM((CHUNKS,) + chunk_of, BF16),
            pltpu.VMEM(chunk_of, F32),
            pltpu.VMEM(chunk_of, BF16),
            pltpu.VMEM((NDP, ROWS // 2, LANES), BF16),
            pltpu.VMEM((NDP - 1, NC * NZ) + chunk_of, BF16),
            pltpu.VMEM((NZ, NX) + chunk_of, BF16),
            pltpu.VMEM((NZ, NX) + chunk_of, F32),
            pltpu.VMEM((NZ, NX) + chunk_of, BF16),
            pltpu.VMEM((NZ,) + chunk_of, BF16),
            pltpu.VMEM((NZ, HALF, LANES), BF16),
            pltpu.VMEM((NZ, HALF, LANES), BF16),
            pltpu.VMEM((NZ,) + chunk_of, BF16),
            pltpu.VMEM((NZ,) + chunk_of, BF16),
            pltpu.VMEM((NZ,) + chunk_of, BF16),
            pltpu.VMEM((NZ,) + chunk_of, BF16),
            pltpu.VMEM((NZ - 1,) + chunk_of, BF16),
            pltpu.VMEM((NZ - 1,) + chunk_of, BF16),
            pltpu.VMEM(chunk_of, F32),
            pltpu.VMEM(chunk_of, BF16),
            pltpu.VMEM(chunk_of, BF16),
            pltpu.VMEM((3 * hid, share), F32),
            pltpu.SemaphoreType.DMA((N_SEMS,)),
        ],
        compiler_params=pltpu.CompilerParams(
            collective_id=0, has_side_effects=True, vmem_limit_bytes=44 * 1024 * 1024
        ),
        name="experts",
    )(tokens, cotangent, route_ids, gates, w_gate, w_up, w_down)


def solution(mesh):
    in_specs = (
        P(("dp", "expert"), "tensor"),
        P(("dp", "expert"), "tensor"),
        P(("dp", "expert"), None),
        P(("dp", "expert"), None),
        P(("expert", "tensor"), None),
        P(("expert", "tensor"), None),
        P(("expert", "tensor"), None),
    )
    out_specs = (
        P(("dp", "expert"), "tensor"),
        P(("dp", "expert"), "tensor"),
        P(("expert", "tensor"), "dp"),
        P(("expert", "tensor"), "dp"),
        P(("expert", "tensor"), "dp"),
    )
    return jax.shard_map(
        per_device, mesh=mesh, in_specs=in_specs, out_specs=out_specs, check_vma=False
    )
```

```python
import jax
import jax.numpy as jnp
from jax import lax
from jax.experimental import pallas as pl
from jax.experimental.pallas import tpu as pltpu
from jax.sharding import PartitionSpec as P

NX, NZ, NC = 4, 4, 2
NY = 8
NDP = 4
CHUNKS = NX * NZ * NC
BLK = 16
ROWS = NY * BLK
REAL = NY * 14
HALF = 64
QUART = ROWS // 4
LANES = 256
HID = 64
N_SEMS = 208
BF16 = jnp.bfloat16
F32 = jnp.float32


def wrap(value, size):
    return lax.rem(value, size)


def nt_dot(left, right):
    return lax.dot_general(left, right, (((1,), (1,)), ((), ())), preferred_element_type=F32)


def tn_dot(left, right):
    return lax.dot_general(left, right, (((0,), (0,)), ((), ())), preferred_element_type=F32)


def kernel(
    tok_in, cot_in, rid_in, gat_in, wg, wu, wd,
    mixed, tgrad, ggrad, ugrad, dgrad,
    tok, cot, rid, gat, wraw, wt, disp, landed, chunk, acc, mine, compact,
    extra, part, kept, sib_in, opp_out, opp_a, opp_b, opp_in, right_out, left_out,
    from_left, from_right, z_out, z_in, total, ret_out, ret, gpart, gbuf, sems, ready,
):
    dp = lax.axis_index("dp")
    y = lax.axis_index("expert")
    t = lax.axis_index("tensor")
    x = t // (NZ * NC)
    z = wrap(t // NC, NZ)
    c = wrap(t, NC)
    other = 1 - c
    xr, xl, xo = wrap(x + 1, NX), wrap(x + 3, NX), wrap(x + 2, NX)
    cols = tok.shape[0]
    count = [0]

    def take(n=1):
        base = count[0]
        count[0] += n
        assert count[0] <= N_SEMS
        return base

    def tensor_at(x_, z_, c_):
        return {"tensor": x_ * (NZ * NC) + z_ * NC + c_}

    def at(c_, x_, z_):
        return c_ * (NX * NZ) + x_ * NZ + z_

    sibling = tensor_at(x, z, other)
    right, left = tensor_at(xr, z, c), tensor_at(xl, z, c)

    def z_peer(k):
        return tensor_at(x, wrap(z + k, NZ), c)

    def y_peer(k):
        return {"expert": wrap(y + k, NY)}

    def dp_peer(k):
        return {"dp": wrap(dp + k, NDP)}

    barrier = pltpu.get_barrier_semaphore()
    partners = [y_peer(k) for k in range(1, NY)]
    partners += [z_peer(k) for k in range(1, NZ)]
    partners += [dp_peer(1), dp_peer(NDP - 1)]
    partners += [sibling, right, left, tensor_at(xo, z, c)]
    for where in partners:
        pl.semaphore_signal(barrier, inc=1, device_id=where, device_id_type=pl.DeviceIdType.MESH)

    def send(src, dst, recv, where):
        copy = pltpu.make_async_remote_copy(
            src_ref=src, dst_ref=dst, send_sem=sems.at[take()], recv_sem=sems.at[recv],
            device_id=where, device_id_type=pl.DeviceIdType.MESH,
        )
        copy.start()
        return copy

    def arrived(ref, sem):
        pltpu.make_async_copy(ref, ref, sems.at[sem]).wait()

    small = []
    for src, dst in ((rid_in, rid), (gat_in, gat), (tok_in, tok), (cot_in, cot)):
        small.append(pltpu.make_async_copy(src, dst, sems.at[take()]))
        small[-1].start()
    loads = []
    for i, ref in enumerate((wg, wu, wd)):
        loads.append(pltpu.make_async_copy(ref, wraw.at[i], sems.at[take()]))
        loads[-1].start()

    lane = lax.broadcasted_iota(jnp.int32, (ROWS, ROWS), 1)
    row = lax.broadcasted_iota(jnp.int32, (ROWS, ROWS), 0)
    label = row // BLK
    first = wrap(row // (BLK // 2), 2) == 0
    slot = wrap(row, BLK // 2)
    upto = jnp.where(row <= lane, 1.0, 0.0).astype(BF16)

    def packed(at_):
        place = wrap(at_, BLK // 2)
        half = wrap(at_ // (BLK // 2), 2)
        return jnp.where(place < 7, (REAL // 2) * half + 7 * (at_ // BLK) + place, -1)

    pack = jnp.where(row == packed(lane), 1.0, 0.0).astype(BF16)
    unpack = jnp.where(lane == packed(row), 1.0, 0.0).astype(BF16)
    disp[...] = jnp.zeros_like(disp)
    small[0].wait()
    small[1].wait()
    hits = jnp.zeros((ROWS, ROWS), F32)
    weight_of = jnp.zeros((ROWS, ROWS), F32)
    for k in range(rid.shape[0]):
        same = rid[k : k + 1, :] == label
        hits = hits + jnp.where(same, 1.0, 0.0)
        weight_of = weight_of + jnp.where(same, gat[k : k + 1, :], 0.0)
    places = jnp.dot(hits.astype(BF16), upto, preferred_element_type=F32) - 1.0
    pick = jnp.where((hits == 1.0) & (places == slot.astype(F32)), 1.0, 0.0)
    slot_gate = jnp.sum(pick * weight_of, axis=1, keepdims=True)
    pick_tok = jnp.where(first, pick, 0.0).astype(BF16)
    pick_cot = jnp.where(first, 0.0, pick).astype(BF16)
    small[2].wait()
    small[3].wait()
    rows_tok = nt_dot(pick_tok, tok[...])
    rows_cot = nt_dot(pick_cot, cot[...])
    disp[:, 0:cols] = (rows_tok + slot_gate * rows_cot).astype(BF16)

    pl.semaphore_wait(barrier, len(partners))
    pl.semaphore_signal(
        ready, inc=1, device_id=dp_peer(NDP - 1), device_id_type=pl.DeviceIdType.MESH
    )

    me = at(c, x, z)
    my_rows = pl.ds(pl.multiple_of(y * BLK, BLK), BLK)
    sent_y = []
    y_in = take(NY - 1)
    for k in range(1, NY):
        there = pl.ds(pl.multiple_of(wrap(y + k, NY) * BLK, BLK), BLK)
        sent_y.append(send(disp.at[there], landed.at[my_rows], y_in + k - 1, y_peer(k)))
    landed[my_rows, :] = disp[my_rows, :]
    chunk[:, REAL:, :] = jnp.zeros((CHUNKS, ROWS - REAL, LANES), BF16)

    for copy in loads:
        copy.wait()
    wt[:, :, LANES // 2 :] = jnp.zeros((CHUNKS, LANES, LANES // 2), BF16)
    wt[:, 3 * HID :, : LANES // 2] = jnp.zeros((CHUNKS, LANES - 3 * HID, LANES // 2), BF16)
    for tt in range(CHUNKS):
        g = at(tt % NC, tt // (NZ * NC), (tt // NC) % NZ)
        for i in range(3):
            wt[g, HID * i : HID * (i + 1), 0:cols] = wraw[i, :, cols * tt : cols * (tt + 1)]
    acc[...] = jnp.zeros_like(acc)

    for k in range(1, NY):
        from_y = pl.ds(pl.multiple_of(wrap(y + NY - k, NY) * BLK, BLK), BLK)
        arrived(landed.at[from_y], y_in + k - 1)
    chunk[me] = jnp.dot(pack, landed[...], preferred_element_type=F32).astype(BF16)

    def consume(g):
        acc[...] += nt_dot(chunk[g], wt[g])

    sib_sem = take(NX * NZ)
    z_sem = take(NZ - 1)
    left_sem, right_sem = take(NZ), take(NZ)
    oa_sem, ob_sem = take(NZ), take(NZ)
    sent_g = []
    sent_q = []
    opposite = tensor_at(xo, z, c)
    straight = (0, NZ - 1)

    def real(g, start=0, size=REAL):
        return chunk.at[g, pl.ds(start, size)]

    def pass_on(ref, sem, where):
        sent_g.append(send(ref, ref, sem, where))

    def to_sibling(x_, k):
        zk = z_at(k)
        pass_on(real(at(c, x_, zk)), sib_sem + x_ * NZ + zk, sibling)
        consume(at(c, x_, zk))

    def sibling_has(x_, k):
        zk = z_at(k)
        g = at(other, x_, zk)
        arrived(real(g), sib_sem + x_ * NZ + zk)
        consume(g)

    def z_at(k):
        return wrap(z + NZ - k, NZ)

    def from_z(k):
        zk = z_at(k)
        g = at(c, x, zk)
        if k > 0:
            arrived(real(g), z_sem + k - 1)
        pass_on(real(g), left_sem + zk, right)
        pass_on(real(g), right_sem + zk, left)
        if k in straight:
            pass_on(real(g), oa_sem + zk, opposite)
        if k == 0:
            for j in range(1, NZ):
                pass_on(real(g), z_sem + j - 1, z_peer(j))
        to_sibling(x, k)

    def from_x(k):
        zk = z_at(k)
        g = at(c, xl, zk)
        arrived(real(g), left_sem + zk)
        if k not in straight:
            pass_on(real(g, 0, HALF), oa_sem + zk, right)
        to_sibling(xl, k)
        g = at(c, xr, zk)
        arrived(real(g), right_sem + zk)
        if k not in straight:
            pass_on(real(g, HALF, REAL - HALF), ob_sem + zk, left)
        to_sibling(xr, k)

    def from_o(k):
        zk = z_at(k)
        g = at(c, xo, zk)
        if k in straight:
            arrived(real(g), oa_sem + zk)
        else:
            arrived(real(g, 0, HALF), oa_sem + zk)
            arrived(real(g, HALF, REAL - HALF), ob_sem + zk)
        to_sibling(xo, k)

    quarter = pl.ds(pl.multiple_of(x * QUART, QUART), QUART)
    q_sem = take(NDP - 1)

    def across():
        pl.semaphore_wait(ready, 1)
        for k in range(1, NDP):
            src = chunk.at[at(c, wrap(dp + k, NDP), z), quarter]
            sent_q.append(send(src, extra.at[k - 1, c * NZ + z, quarter], q_sem + k - 1, dp_peer(k)))

    from_z(0)
    from_z(1)
    from_x(0)
    sibling_has(x, 0)
    from_z(2)
    from_o(0)
    across()
    from_x(1)
    sibling_has(x, 1)
    from_z(3)
    sibling_has(xl, 0)
    sibling_has(xr, 0)
    from_x(2)
    sibling_has(x, 2)
    sibling_has(xo, 0)
    from_o(1)
    sibling_has(xl, 1)
    sibling_has(xr, 1)
    sibling_has(x, 3)
    from_x(3)
    sibling_has(xl, 2)
    sibling_has(xr, 2)
    from_o(2)
    sibling_has(xo, 1)
    from_o(3)
    sibling_has(xl, 3)
    sibling_has(xr, 3)
    sibling_has(xo, 2)
    sibling_has(xo, 3)

    half_rows = REAL // 2
    fwd = acc[:half_rows, : 2 * HID]
    bwd = acc[half_rows:REAL, 2 * HID :]
    low = lax.broadcasted_iota(jnp.int32, (half_rows, 2 * HID), 1) < HID
    turned = pltpu.roll(fwd, HID, 1)
    pre = jnp.where(low, fwd, turned)
    upper = jnp.where(low, turned, fwd)
    back = bwd + pltpu.roll(bwd, HID, 1)
    sig = jax.nn.sigmoid(pre)
    act = pre * sig
    hidden = act * upper
    gate_delta = back * upper * sig * (1.0 + pre * (1.0 - sig))
    up_delta = back * act
    deltas = jnp.where(low, gate_delta, up_delta)
    hid = jnp.where(low, hidden, 0.0)
    zeros = jnp.zeros((half_rows, 2 * HID), F32)
    pad = jnp.zeros((ROWS // 2 - half_rows, LANES), F32)
    tail = jnp.zeros((ROWS - REAL, LANES), F32)
    compact[NDP - 1] = jnp.concatenate(
        [jnp.concatenate([deltas, hid], axis=1), pad], axis=0
    ).astype(BF16)
    top = jnp.concatenate([zeros, hid], axis=1)
    bottom = jnp.concatenate([deltas, zeros], axis=1)
    mine[...] = jnp.concatenate([top, bottom, tail], axis=0).astype(BF16)

    m_sem = take(NDP - 1)
    sent_m = []
    for k in range(1, NDP):
        sent_m.append(send(compact.at[NDP - 1], compact.at[k - 1], m_sem + k - 1, dp_peer(k)))

    sr_sem = take(NZ)
    xa_sem, xb_sem = take(NZ), take(NZ)
    nl_sem, nr_sem = take(NZ), take(NZ)
    zr_sem = take(NZ - 1)
    sent_r = []

    def stage_a(k):
        zk = wrap(z + k + 1, NZ)
        left_side = mine[...]

        def one(x_, carry):
            part[k, x_] = jnp.dot(
                left_side, wt[at(other, x_, zk)], preferred_element_type=F32
            ).astype(BF16)
            return carry

        lax.fori_loop(0, NX, one, 0)
        rows = pl.ds(0, REAL)
        sent_r.append(send(part.at[k, :, rows], sib_in.at[k, :, rows], sr_sem + k, sibling))

        def two(x_, carry):
            kept[k, x_] = jnp.dot(left_side, wt[at(c, x_, zk)], preferred_element_type=F32)
            return carry

        lax.fori_loop(0, NX, two, 0)

    def pair(k, x_):
        return kept[k, x_, :REAL] + sib_in[k, x_, :REAL].astype(F32)

    def stage_b(k):
        arrived(sib_in.at[k, :, pl.ds(0, REAL)], sr_sem + k)
        opp_out[k] = pair(k, xo).astype(BF16)
        if k in straight:
            sent_r.append(send(opp_out.at[k], opp_in.at[k // (NZ - 1)], xa_sem + k, opposite))
            return
        sent_r.append(send(opp_out.at[k, pl.ds(0, HALF)], opp_a.at[k], xa_sem + k, right))
        sent_r.append(send(opp_out.at[k, pl.ds(HALF, REAL - HALF)], opp_b.at[k], xb_sem + k, left))

    def stage_c(k):
        value = pair(k, xr)
        if k in straight:
            right_out[k] = value.astype(BF16)
        else:
            arrived(opp_a.at[k], xa_sem + k)
            right_out[k, :HALF] = (value[:HALF] + opp_a[k].astype(F32)).astype(BF16)
            right_out[k, HALF:] = value[HALF:].astype(BF16)
        sent_r.append(send(right_out.at[k], from_left.at[k], nl_sem + k, right))
        value = pair(k, xl)
        if k in straight:
            left_out[k] = value.astype(BF16)
        else:
            arrived(opp_b.at[k], xb_sem + k)
            left_out[k, :HALF] = value[:HALF].astype(BF16)
            left_out[k, HALF:] = (value[HALF:] + opp_b[k].astype(F32)).astype(BF16)
        sent_r.append(send(left_out.at[k], from_right.at[k], nr_sem + k, left))

    def stage_d(k):
        arrived(from_left.at[k], nl_sem + k)
        arrived(from_right.at[k], nr_sem + k)
        value = pair(k, x) + from_left[k].astype(F32) + from_right[k].astype(F32)
        if k in straight:
            arrived(opp_in.at[k // (NZ - 1)], xa_sem + k)
            value = value + opp_in[k // (NZ - 1)].astype(F32)
        if k < NZ - 1:
            z_out[k] = value.astype(BF16)
            sent_r.append(send(z_out.at[k], z_in.at[k], zr_sem + k, z_peer(k + 1)))
        else:
            total[...] = value

    qz_sem = take(NZ - 1)
    ql_sem, qr_sem, qa_sem, qb_sem = take(NZ), take(NZ), take(NZ), take(NZ)
    qs_sem = take(NZ)

    def part_rows(x_, start, size):
        return pl.ds(pl.multiple_of(x_ * QUART + start, BLK), size)

    def spread_1():
        for k in range(1, NDP):
            arrived(extra.at[k - 1, c * NZ + z, quarter], q_sem + k - 1)
        piece = extra.at[:, c * NZ + z, quarter]
        for k in range(1, NZ):
            sent_q.append(send(piece, piece, qz_sem + k - 1, z_peer(k)))
        sent_q.append(send(piece, piece, ql_sem + 0, right))
        sent_q.append(send(piece, piece, qr_sem + 0, left))

    def spread_2(k):
        piece = extra.at[:, c * NZ + z_at(k), quarter]
        arrived(piece, qz_sem + k - 1)
        sent_q.append(send(piece, piece, ql_sem + k, right))
        sent_q.append(send(piece, piece, qr_sem + k, left))

    def spread_3(k):
        here = c * NZ + z_at(k)
        arrived(extra.at[:, here, part_rows(xl, 0, QUART)], ql_sem + k)
        piece = extra.at[:, here, part_rows(xl, 0, QUART // 2)]
        sent_q.append(send(piece, piece, qa_sem + k, right))
        arrived(extra.at[:, here, part_rows(xr, 0, QUART)], qr_sem + k)
        piece = extra.at[:, here, part_rows(xr, QUART // 2, QUART // 2)]
        sent_q.append(send(piece, piece, qb_sem + k, left))

    def spread_4(k):
        here = c * NZ + z_at(k)
        arrived(extra.at[:, here, part_rows(xo, 0, QUART // 2)], qa_sem + k)
        arrived(extra.at[:, here, part_rows(xo, QUART // 2, QUART // 2)], qb_sem + k)
        piece = extra.at[:, here]
        sent_q.append(send(piece, piece, qs_sem + k, sibling))

    stage_a(0)
    stage_a(1)
    stage_b(0)
    stage_c(0)
    stage_a(2)
    stage_b(1)
    spread_1()
    stage_a(3)
    stage_b(2)
    stage_c(1)
    stage_d(0)
    stage_c(2)
    stage_d(1)
    spread_2(1)
    stage_b(3)
    stage_c(3)
    spread_3(0)
    spread_2(2)
    spread_2(3)
    stage_d(2)
    stage_d(3)

    value = total[...]
    for k in range(NZ - 1):
        arrived(z_in.at[k], zr_sem + k)
        value = value + z_in[k].astype(F32)
    ret_out[...] = jnp.dot(
        unpack[:, :REAL], value.astype(BF16), preferred_element_type=F32
    ).astype(BF16)

    yr_sem = take(NY - 1)
    for k in range(1, NY):
        there = pl.ds(pl.multiple_of(wrap(y + k, NY) * BLK, BLK), BLK)
        sent_r.append(send(ret_out.at[there], ret.at[my_rows], yr_sem + k - 1, y_peer(k)))
    ret[my_rows, :] = ret_out[my_rows, :]
    spread_4(0)
    for k in range(1, NZ):
        spread_3(k)
    for k in range(1, NZ):
        spread_4(k)

    for k in range(1, NDP):
        arrived(compact.at[k - 1], m_sem + k - 1)
    sides = []
    for k in range(NDP):
        both = compact[k, :half_rows].astype(F32)
        top = jnp.concatenate([both[:, : 2 * HID], zeros], axis=1)
        bottom = jnp.concatenate([zeros, both[:, 2 * HID :]], axis=1)
        side = jnp.concatenate([top, bottom, tail], axis=0)
        sides.append(jnp.transpose(side)[: 3 * HID].astype(BF16))
    def gradient(k):
        z_ = z_at(k)
        arrived(extra.at[:, other * NZ + z_], qs_sem + k)
        for c_ in range(NC):
            value = jnp.dot(sides[NDP - 1], chunk[at(c_, dp, z_)], preferred_element_type=F32)
            for j in range(1, NDP):
                value += jnp.dot(
                    sides[j - 1], extra[j - 1, c_ * NZ + z_], preferred_element_type=F32
                )
            gpart[z_ * NC + c_] = value

    for copy in sent_y + sent_g:
        copy.wait_send()
    gradient(0)
    gradient(1)
    gradient(2)

    gate_of = jnp.where(first, pick * weight_of, 0.0)
    high = gate_of.astype(BF16)
    low_part = (gate_of - high.astype(F32)).astype(BF16)
    for k in range(1, NY):
        from_y = pl.ds(pl.multiple_of(wrap(y + NY - k, NY) * BLK, BLK), BLK)
        arrived(ret.at[from_y], yr_sem + k - 1)
    got = ret[...]
    out = tn_dot(got, high) + tn_dot(got, low_part)
    mixed[...] = out[:cols].astype(BF16)
    tgrad[...] = tn_dot(got, pick_cot)[:cols].astype(BF16)

    gradient(3)
    gbuf[...] = jnp.zeros_like(gbuf)
    for i in range(NZ * NC):
        start = cols * i // 128 * 128
        shift = cols * i - start
        width = min(LANES + 128, gbuf.shape[1] - start)
        wide = gpart[i]
        if width > LANES:
            wide = jnp.concatenate([wide, jnp.zeros((3 * HID, width - LANES), F32)], axis=1)
        if shift:
            wide = pltpu.roll(wide, shift, 1)
        gbuf[:, start : start + width] += wide
    ggrad[...] = gbuf[:HID].astype(BF16)
    ugrad[...] = gbuf[HID : 2 * HID].astype(BF16)
    dgrad[...] = gbuf[2 * HID :].astype(BF16)

    for copy in sent_q + sent_m + sent_r:
        copy.wait_send()


def write_out(*refs):
    count = len(refs) // 2
    sems = refs[-1]
    copies = [
        pltpu.make_async_copy(refs[i], refs[count + i], sems.at[i]) for i in range(count)
    ]
    for copy in copies:
        copy.start()
    for copy in copies:
        copy.wait()


def per_device(tokens, cotangent, route_ids, gates, w_gate, w_up, w_down):
    rows, cols = tokens.shape
    hid, width = w_gate.shape
    share = width // NDP
    top = route_ids.shape[1]
    vmem = pl.BlockSpec(memory_space=pltpu.VMEM)
    hbm = pl.BlockSpec(memory_space=pl.ANY)
    chunk_of = (ROWS, LANES)
    real_of = (REAL, LANES)
    shapes = (
        jax.ShapeDtypeStruct((cols, rows), BF16),
        jax.ShapeDtypeStruct((cols, rows), BF16),
        jax.ShapeDtypeStruct((hid, share), BF16),
        jax.ShapeDtypeStruct((hid, share), BF16),
        jax.ShapeDtypeStruct((hid, share), BF16),
    )
    operands = (tokens.T, cotangent.T, route_ids.T, gates.T, w_gate, w_up, w_down)
    results = pl.pallas_call(
        kernel,
        out_shape=shapes,
        in_specs=[hbm] * 7,
        out_specs=[vmem] * 5,
        scratch_shapes=[
            pltpu.VMEM((cols, rows), BF16),
            pltpu.VMEM((cols, rows), BF16),
            pltpu.VMEM((top, rows), jnp.int32),
            pltpu.VMEM((top, rows), F32),
            pltpu.VMEM((3, hid, width), BF16),
            pltpu.VMEM((CHUNKS, LANES, LANES), BF16),
            pltpu.VMEM(chunk_of, BF16),
            pltpu.VMEM(chunk_of, BF16),
            pltpu.VMEM((CHUNKS,) + chunk_of, BF16),
            pltpu.VMEM(chunk_of, F32),
            pltpu.VMEM(chunk_of, BF16),
            pltpu.VMEM((NDP, ROWS // 2, LANES), BF16),
            pltpu.VMEM((NDP - 1, NC * NZ) + chunk_of, BF16),
            pltpu.VMEM((NZ, NX) + chunk_of, BF16),
            pltpu.VMEM((NZ, NX) + chunk_of, F32),
            pltpu.VMEM((NZ, NX) + chunk_of, BF16),
            pltpu.VMEM((NZ,) + real_of, BF16),
            pltpu.VMEM((NZ, HALF, LANES), BF16),
            pltpu.VMEM((NZ, REAL - HALF, LANES), BF16),
            pltpu.VMEM((2,) + real_of, BF16),
            pltpu.VMEM((NZ,) + real_of, BF16),
            pltpu.VMEM((NZ,) + real_of, BF16),
            pltpu.VMEM((NZ,) + real_of, BF16),
            pltpu.VMEM((NZ,) + real_of, BF16),
            pltpu.VMEM((NZ - 1,) + real_of, BF16),
            pltpu.VMEM((NZ - 1,) + real_of, BF16),
            pltpu.VMEM(real_of, F32),
            pltpu.VMEM(chunk_of, BF16),
            pltpu.VMEM(chunk_of, BF16),
            pltpu.VMEM((NZ * NC, 3 * hid, LANES), F32),
            pltpu.VMEM((3 * hid, share), F32),
            pltpu.SemaphoreType.DMA((N_SEMS,)),
            pltpu.SemaphoreType.REGULAR,
        ],
        compiler_params=pltpu.CompilerParams(
            collective_id=0, has_side_effects=True, vmem_limit_bytes=40 * 1024 * 1024
        ),
        name="experts",
    )(*[pltpu.with_memory_space_constraint(v, pltpu.HBM) for v in operands])
    results = pl.pallas_call(
        write_out,
        out_shape=shapes,
        in_specs=[vmem] * 5,
        out_specs=[hbm] * 5,
        scratch_shapes=[pltpu.SemaphoreType.DMA((5,))],
        compiler_params=pltpu.CompilerParams(vmem_limit_bytes=40 * 1024 * 1024),
        name="write_out",
    )(*results)
    return (results[0].T, results[1].T) + tuple(results[2:])


def solution(mesh):
    in_specs = (
        P(("dp", "expert"), "tensor"),
        P(("dp", "expert"), "tensor"),
        P(("dp", "expert"), None),
        P(("dp", "expert"), None),
        P(("expert", "tensor"), None),
        P(("expert", "tensor"), None),
        P(("expert", "tensor"), None),
    )
    out_specs = (
        P(("dp", "expert"), "tensor"),
        P(("dp", "expert"), "tensor"),
        P(("expert", "tensor"), "dp"),
        P(("expert", "tensor"), "dp"),
        P(("expert", "tensor"), "dp"),
    )
    return jax.shard_map(
        per_device, mesh=mesh, in_specs=in_specs, out_specs=out_specs, check_vma=False
    )
```

```python
import jax
import jax.numpy as jnp
from jax import lax
from jax.experimental import pallas as pl
from jax.experimental.pallas import tpu as pltpu
from jax.sharding import PartitionSpec as P

NX, NZ, NC = 4, 4, 2
NY = 8
NDP = 4
CHUNKS = NX * NZ * NC
BLK = 16
ROWS = NY * BLK
REAL = NY * 14
HALF = 64
QUART = ROWS // 4
LANES = 256
HID = 64
N_SEMS = 240
BF16 = jnp.bfloat16
F32 = jnp.float32


def wrap(value, size):
    return lax.rem(value, size)


def nt_dot(left, right):
    return lax.dot_general(left, right, (((1,), (1,)), ((), ())), preferred_element_type=F32)


def tn_dot(left, right):
    return lax.dot_general(left, right, (((0,), (0,)), ((), ())), preferred_element_type=F32)


def kernel(
    tok_in, cot_in, rid_in, gat_in, wg, wu, wd,
    mixed, tgrad, ggrad, ugrad, dgrad,
    tok, cot, rid, gat, wraw, wt, disp, landed, chunk, acc, acc_sib, acc_in, mine, theirs, wsib, compact,
    extra, kept, opp_out, opp_a, opp_b, opp_in, right_out, left_out,
    from_left, from_right, z_out, z_in, total, ret_out, ret, gpart, gbuf, sems, ready,
):
    dp = lax.axis_index("dp")
    y = lax.axis_index("expert")
    t = lax.axis_index("tensor")
    x = t // (NZ * NC)
    z = wrap(t // NC, NZ)
    c = wrap(t, NC)
    other = 1 - c
    xr, xl, xo = wrap(x + 1, NX), wrap(x + 3, NX), wrap(x + 2, NX)
    cols = tok.shape[0]
    count = [0]

    def take(n=1):
        base = count[0]
        count[0] += n
        assert count[0] <= N_SEMS
        return base

    def tensor_at(x_, z_, c_):
        return {"tensor": x_ * (NZ * NC) + z_ * NC + c_}

    def at(c_, x_, z_):
        return c_ * (NX * NZ) + x_ * NZ + z_

    upper_z = z // 2

    def z_at(k):
        return (z, 1 - z + 4 * upper_z, 2 - upper_z, 3 - 3 * upper_z)[k]

    sibling = tensor_at(x, z, other)
    right, left = tensor_at(xr, z, c), tensor_at(xl, z, c)

    def z_peer(k):
        return tensor_at(x, z_at(k), c)

    def y_peer(k):
        return {"expert": wrap(y + k, NY)}

    def dp_peer(k):
        return {"dp": wrap(dp + k, NDP)}

    barrier = pltpu.get_barrier_semaphore()
    partners = [y_peer(k) for k in range(1, NY)]
    partners += [z_peer(k) for k in range(1, NZ)]
    partners += [dp_peer(1), dp_peer(NDP - 1)]
    partners += [sibling, right, left, tensor_at(xo, z, c)]
    for where in partners:
        pl.semaphore_signal(barrier, inc=1, device_id=where, device_id_type=pl.DeviceIdType.MESH)

    def send(src, dst, recv, where):
        copy = pltpu.make_async_remote_copy(
            src_ref=src, dst_ref=dst, send_sem=sems.at[take()], recv_sem=sems.at[recv],
            device_id=where, device_id_type=pl.DeviceIdType.MESH,
        )
        copy.start()
        return copy

    def arrived(ref, sem):
        pltpu.make_async_copy(ref, ref, sems.at[sem]).wait()

    small = []
    for src, dst in ((rid_in, rid), (gat_in, gat), (tok_in, tok), (cot_in, cot)):
        small.append(pltpu.make_async_copy(src, dst, sems.at[take()]))
        small[-1].start()
    loads = []
    for i, ref in enumerate((wg, wu, wd)):
        loads.append(pltpu.make_async_copy(ref, wraw.at[i], sems.at[take()]))
        loads[-1].start()

    lane = lax.broadcasted_iota(jnp.int32, (ROWS, ROWS), 1)
    row = lax.broadcasted_iota(jnp.int32, (ROWS, ROWS), 0)
    label = row // BLK
    first = wrap(row // (BLK // 2), 2) == 0
    slot = wrap(row, BLK // 2)
    upto = jnp.where(row <= lane, 1.0, 0.0).astype(BF16)

    def packed(at_):
        place = wrap(at_, BLK // 2)
        half = wrap(at_ // (BLK // 2), 2)
        return jnp.where(place < 7, (REAL // 2) * half + 7 * (at_ // BLK) + place, -1)

    pack = jnp.where(row == packed(lane), 1.0, 0.0).astype(BF16)
    unpack = jnp.where(lane == packed(row), 1.0, 0.0).astype(BF16)
    disp[...] = jnp.zeros_like(disp)
    small[0].wait()
    small[1].wait()
    hits = jnp.zeros((ROWS, ROWS), F32)
    weight_of = jnp.zeros((ROWS, ROWS), F32)
    for k in range(rid.shape[0]):
        same = rid[k : k + 1, :] == label
        hits = hits + jnp.where(same, 1.0, 0.0)
        weight_of = weight_of + jnp.where(same, gat[k : k + 1, :], 0.0)
    places = jnp.dot(hits.astype(BF16), upto, preferred_element_type=F32) - 1.0
    pick = jnp.where((hits == 1.0) & (places == slot.astype(F32)), 1.0, 0.0)
    slot_gate = jnp.sum(pick * weight_of, axis=1, keepdims=True)
    pick_tok = jnp.where(first, pick, 0.0).astype(BF16)
    pick_cot = jnp.where(first, 0.0, pick).astype(BF16)
    small[2].wait()
    small[3].wait()
    rows_tok = nt_dot(pick_tok, tok[...])
    rows_cot = nt_dot(pick_cot, cot[...])
    disp[:, 0:cols] = (rows_tok + slot_gate * rows_cot).astype(BF16)

    pl.semaphore_wait(barrier, len(partners))
    pl.semaphore_signal(
        ready, inc=1, device_id=dp_peer(NDP - 1), device_id_type=pl.DeviceIdType.MESH
    )

    me = at(c, x, z)
    my_rows = pl.ds(pl.multiple_of(y * BLK, BLK), BLK)
    sent_y = []
    y_in = take(NY - 1)
    for k in range(1, NY):
        there = pl.ds(pl.multiple_of(wrap(y + k, NY) * BLK, BLK), BLK)
        sent_y.append(send(disp.at[there], landed.at[my_rows], y_in + k - 1, y_peer(k)))
    landed[my_rows, :] = disp[my_rows, :]
    chunk[:, REAL:, :] = jnp.zeros((CHUNKS, ROWS - REAL, LANES), BF16)

    for copy in loads:
        copy.wait()
    wt[:, :, LANES // 2 :] = jnp.zeros((CHUNKS, LANES, LANES // 2), BF16)
    wt[:, 3 * HID :, : LANES // 2] = jnp.zeros((CHUNKS, LANES - 3 * HID, LANES // 2), BF16)
    for tt in range(CHUNKS):
        g = at(tt % NC, tt // (NZ * NC), (tt // NC) % NZ)
        for i in range(3):
            wt[g, HID * i : HID * (i + 1), 0:cols] = wraw[i, :, cols * tt : cols * (tt + 1)]
    acc[...] = jnp.zeros_like(acc)
    acc_sib[...] = jnp.zeros_like(acc_sib)
    wsib[:, 3 * HID :, :] = jnp.zeros((NX * NZ, LANES - 3 * HID, LANES), BF16)
    w_sem = take()
    held = pl.ds(0, 3 * HID)
    give = pl.ds(pl.multiple_of(other * (NX * NZ), NX * NZ), NX * NZ)
    sent_w = [send(wt.at[give, held], wsib.at[:, held], w_sem, sibling)]

    for k in range(1, NY):
        from_y = pl.ds(pl.multiple_of(wrap(y + NY - k, NY) * BLK, BLK), BLK)
        arrived(landed.at[from_y], y_in + k - 1)
    chunk[me] = jnp.dot(pack, landed[...], preferred_element_type=F32).astype(BF16)

    def consume(x_, k):
        zk = z_at(k)
        g = at(c, x_, zk)
        value = chunk[g]
        acc[...] += nt_dot(value, wt[g])
        acc_sib[...] += nt_dot(value, wsib[x_ * NZ + zk])

    z_sem = take(NZ)
    left_sem, right_sem = take(NZ), take(NZ)
    oa_sem, ob_sem = take(NZ), take(NZ)
    sent_g = []
    sent_q = []
    opposite = tensor_at(xo, z, c)
    straight = (0, NZ - 1)

    def real(g, start=0, size=REAL):
        return chunk.at[g, pl.ds(start, size)]

    def pass_on(ref, sem, where):
        sent_g.append(send(ref, ref, sem, where))

    def from_z(k):
        zk = z_at(k)
        g = at(c, x, zk)
        if k > 0:
            arrived(real(g), z_sem + zk)
        pass_on(real(g), left_sem + zk, right)
        pass_on(real(g), right_sem + zk, left)
        if k in straight:
            pass_on(real(g), oa_sem + zk, opposite)
        if k == 0:
            for j in range(1, NZ):
                pass_on(real(g), z_sem + z, z_peer(j))

    def from_x(k):
        zk = z_at(k)
        g = at(c, xl, zk)
        arrived(real(g), left_sem + zk)
        if k not in straight:
            pass_on(real(g, 0, HALF), oa_sem + zk, right)
        g = at(c, xr, zk)
        arrived(real(g), right_sem + zk)
        if k not in straight:
            pass_on(real(g, HALF, REAL - HALF), ob_sem + zk, left)

    def from_o(k):
        zk = z_at(k)
        g = at(c, xo, zk)
        if k in straight:
            arrived(real(g), oa_sem + zk)
        else:
            arrived(real(g, 0, HALF), oa_sem + zk)
            arrived(real(g, HALF, REAL - HALF), ob_sem + zk)

    quarter = pl.ds(pl.multiple_of(x * QUART, QUART), QUART)
    q_sem = take(NDP - 1)

    def across():
        pl.semaphore_wait(ready, 1)
        for k in range(1, NDP):
            src = chunk.at[at(c, wrap(dp + k, NDP), z), quarter]
            sent_q.append(send(src, extra.at[k - 1, c * NZ + z, quarter], q_sem + k - 1, dp_peer(k)))

    from_z(0)
    from_z(1)
    from_x(0)
    from_z(2)
    from_o(0)
    across()
    from_x(1)
    arrived(wsib.at[:, held], w_sem)
    consume(x, 0)
    consume(x, 1)
    from_z(3)
    consume(xl, 0)
    consume(xr, 0)
    consume(x, 2)
    from_x(2)
    consume(xo, 0)
    consume(xl, 1)
    consume(xr, 1)
    from_o(1)
    consume(x, 3)
    consume(xl, 2)
    consume(xr, 2)
    from_x(3)
    consume(xo, 1)
    from_o(2)
    consume(xl, 3)
    consume(xr, 3)
    consume(xo, 2)
    from_o(3)
    consume(xo, 3)

    acc_sem, slots_sem, theirs_sem = take(), take(), take()
    own_rows = pl.ds(0, REAL)
    sent_w.append(send(acc_sib.at[own_rows], acc_in, acc_sem, sibling))
    mine_at = pl.ds(pl.multiple_of(c * (NX * NZ) + dp * NZ, NZ), NZ)
    other_at = pl.ds(pl.multiple_of(other * (NX * NZ) + dp * NZ, NZ), NZ)
    slots = chunk.at[mine_at, own_rows]
    sent_w.append(send(slots, slots, slots_sem, sibling))
    arrived(acc_in, acc_sem)
    acc[:REAL] += acc_in[...]

    half_rows = REAL // 2
    fwd = acc[:half_rows, : 2 * HID]
    bwd = acc[half_rows:REAL, 2 * HID :]
    low = lax.broadcasted_iota(jnp.int32, (half_rows, 2 * HID), 1) < HID
    turned = pltpu.roll(fwd, HID, 1)
    pre = jnp.where(low, fwd, turned)
    upper = jnp.where(low, turned, fwd)
    back = bwd + pltpu.roll(bwd, HID, 1)
    sig = jax.nn.sigmoid(pre)
    act = pre * sig
    hidden = act * upper
    gate_delta = back * upper * sig * (1.0 + pre * (1.0 - sig))
    up_delta = back * act
    deltas = jnp.where(low, gate_delta, up_delta)
    hid = jnp.where(low, hidden, 0.0)
    zeros = jnp.zeros((half_rows, 2 * HID), F32)
    pad = jnp.zeros((ROWS // 2 - half_rows, LANES), F32)
    tail = jnp.zeros((ROWS - REAL, LANES), F32)
    top = jnp.concatenate([zeros, hid], axis=1)
    bottom = jnp.concatenate([deltas, zeros], axis=1)
    mine[...] = jnp.concatenate([top, bottom, tail], axis=0).astype(BF16)

    sent_w.append(send(mine, theirs, theirs_sem, sibling))
    compact[NDP - 1] = jnp.concatenate(
        [jnp.concatenate([deltas, hid], axis=1), pad], axis=0
    ).astype(BF16)
    m_sem = take(NDP - 1)
    sent_m = []
    for k in range(1, NDP):
        sent_m.append(send(compact.at[NDP - 1], compact.at[k - 1], m_sem + k - 1, dp_peer(k)))

    xa_sem, xb_sem = take(NZ), take(NZ)
    nl_sem, nr_sem = take(NZ), take(NZ)
    zr_sem = take(NZ)
    sent_r = []

    def stage_a(k):
        zk = z_at(NZ - 1 - k) if k < NZ - 1 else z
        ours, other_side = mine[...], theirs[...]

        def one(x_, carry):
            kept[k, x_] = jnp.dot(ours, wt[at(c, x_, zk)], preferred_element_type=F32) + jnp.dot(
                other_side, wsib[x_ * NZ + zk], preferred_element_type=F32
            )
            return carry

        lax.fori_loop(0, NX, one, 0)

    def pair(k, x_):
        return kept[k, x_, :REAL]

    def stage_b(k):
        opp_out[k] = pair(k, xo).astype(BF16)
        if k in straight:
            sent_r.append(send(opp_out.at[k], opp_in.at[k // (NZ - 1)], xa_sem + k, opposite))
            return
        sent_r.append(send(opp_out.at[k, pl.ds(0, HALF)], opp_a.at[k], xa_sem + k, right))
        sent_r.append(send(opp_out.at[k, pl.ds(HALF, REAL - HALF)], opp_b.at[k], xb_sem + k, left))

    def stage_c(k):
        value = pair(k, xr)
        if k in straight:
            right_out[k] = value.astype(BF16)
        else:
            arrived(opp_a.at[k], xa_sem + k)
            right_out[k, :HALF] = (value[:HALF] + opp_a[k].astype(F32)).astype(BF16)
            right_out[k, HALF:] = value[HALF:].astype(BF16)
        sent_r.append(send(right_out.at[k], from_left.at[k], nl_sem + k, right))
        value = pair(k, xl)
        if k in straight:
            left_out[k] = value.astype(BF16)
        else:
            arrived(opp_b.at[k], xb_sem + k)
            left_out[k, :HALF] = value[:HALF].astype(BF16)
            left_out[k, HALF:] = (value[HALF:] + opp_b[k].astype(F32)).astype(BF16)
        sent_r.append(send(left_out.at[k], from_right.at[k], nr_sem + k, left))

    def stage_d(k):
        arrived(from_left.at[k], nl_sem + k)
        arrived(from_right.at[k], nr_sem + k)
        value = pair(k, x) + from_left[k].astype(F32) + from_right[k].astype(F32)
        if k in straight:
            arrived(opp_in.at[k // (NZ - 1)], xa_sem + k)
            value = value + opp_in[k // (NZ - 1)].astype(F32)
        if k < NZ - 1:
            z_out[k] = value.astype(BF16)
            sent_r.append(send(z_out.at[k], z_in.at[z], zr_sem + z, z_peer(NZ - 1 - k)))
        else:
            total[...] = value

    qz_sem = take(NZ)
    ql_sem, qr_sem, qa_sem, qb_sem = take(NZ), take(NZ), take(NZ), take(NZ)
    qs_sem = take(NZ)

    def part_rows(x_, start, size):
        return pl.ds(pl.multiple_of(x_ * QUART + start, BLK), size)

    def spread_1():
        for k in range(1, NDP):
            arrived(extra.at[k - 1, c * NZ + z, quarter], q_sem + k - 1)
        piece = extra.at[:, c * NZ + z, quarter]
        for k in range(1, NZ):
            sent_q.append(send(piece, piece, qz_sem + z, z_peer(k)))
        sent_q.append(send(piece, piece, ql_sem + 0, right))
        sent_q.append(send(piece, piece, qr_sem + 0, left))

    def spread_2(k):
        piece = extra.at[:, c * NZ + z_at(k), quarter]
        arrived(piece, qz_sem + z_at(k))
        sent_q.append(send(piece, piece, ql_sem + k, right))
        sent_q.append(send(piece, piece, qr_sem + k, left))

    def spread_3(k):
        here = c * NZ + z_at(k)
        arrived(extra.at[:, here, part_rows(xl, 0, QUART)], ql_sem + k)
        piece = extra.at[:, here, part_rows(xl, 0, QUART // 2)]
        sent_q.append(send(piece, piece, qa_sem + k, right))
        arrived(extra.at[:, here, part_rows(xr, 0, QUART)], qr_sem + k)
        piece = extra.at[:, here, part_rows(xr, QUART // 2, QUART // 2)]
        sent_q.append(send(piece, piece, qb_sem + k, left))

    def spread_4(k):
        here = c * NZ + z_at(k)
        arrived(extra.at[:, here, part_rows(xo, 0, QUART // 2)], qa_sem + k)
        arrived(extra.at[:, here, part_rows(xo, QUART // 2, QUART // 2)], qb_sem + k)
        piece = extra.at[:, here]
        sent_q.append(send(piece, piece, qs_sem + k, sibling))

    arrived(theirs, theirs_sem)
    stage_a(0)
    stage_b(0)
    stage_c(0)
    stage_a(1)
    stage_b(1)
    stage_a(2)
    stage_b(2)
    spread_1()
    stage_c(1)
    stage_a(3)
    stage_d(0)
    stage_c(2)
    stage_d(1)
    spread_2(1)
    stage_b(3)
    stage_c(3)
    spread_3(0)
    spread_2(2)
    spread_2(3)
    stage_d(2)
    stage_d(3)

    value = total[...]
    for k in range(1, NZ):
        arrived(z_in.at[z_at(k)], zr_sem + z_at(k))
        value = value + z_in[z_at(k)].astype(F32)
    ret_out[...] = jnp.dot(
        unpack[:, :REAL], value.astype(BF16), preferred_element_type=F32
    ).astype(BF16)

    yr_sem = take(NY - 1)
    sent_b = []
    for k in range(1, NY):
        there = pl.ds(pl.multiple_of(wrap(y + k, NY) * BLK, BLK), BLK)
        sent_b.append(send(ret_out.at[there], ret.at[my_rows], yr_sem + k - 1, y_peer(k)))
    ret[my_rows, :] = ret_out[my_rows, :]
    spread_4(0)
    for k in range(1, NZ):
        spread_3(k)
    for k in range(1, NZ):
        spread_4(k)

    for k in range(1, NDP):
        arrived(compact.at[k - 1], m_sem + k - 1)
    sides = []
    for k in range(NDP):
        both = compact[k, :half_rows].astype(F32)
        top = jnp.concatenate([both[:, : 2 * HID], zeros], axis=1)
        bottom = jnp.concatenate([zeros, both[:, 2 * HID :]], axis=1)
        side = jnp.concatenate([top, bottom, tail], axis=0)
        sides.append(jnp.transpose(side)[: 3 * HID].astype(BF16))
    def gradient(k):
        z_ = z_at(k)
        arrived(extra.at[:, other * NZ + z_], qs_sem + k)
        for c_ in range(NC):
            value = jnp.dot(sides[NDP - 1], chunk[at(c_, dp, z_)], preferred_element_type=F32)
            for j in range(1, NDP):
                value += jnp.dot(
                    sides[j - 1], extra[j - 1, c_ * NZ + z_], preferred_element_type=F32
                )
            gpart[z_ * NC + c_] = value

    for copy in sent_y + sent_g + sent_m + sent_r + sent_w:
        copy.wait_send()
    arrived(chunk.at[other_at, own_rows], slots_sem)
    gradient(0)
    gradient(1)
    gradient(2)

    gate_of = jnp.where(first, pick * weight_of, 0.0)
    high = gate_of.astype(BF16)
    low_part = (gate_of - high.astype(F32)).astype(BF16)
    back_to = jnp.concatenate([high, low_part, pick_cot], axis=1)
    for k in range(1, NY):
        from_y = pl.ds(pl.multiple_of(wrap(y + NY - k, NY) * BLK, BLK), BLK)
        arrived(ret.at[from_y], yr_sem + k - 1)
    got = ret[...]
    out = tn_dot(got, back_to)[:cols]
    mixed[...] = (out[:, :ROWS] + out[:, ROWS : 2 * ROWS]).astype(BF16)
    tgrad[...] = out[:, 2 * ROWS :].astype(BF16)

    gradient(3)
    gbuf[...] = jnp.zeros_like(gbuf)
    for i in range(NZ * NC):
        start = cols * i // 128 * 128
        shift = cols * i - start
        width = min(LANES + 128, gbuf.shape[1] - start)
        wide = gpart[i]
        if width > LANES:
            wide = jnp.concatenate([wide, jnp.zeros((3 * HID, width - LANES), F32)], axis=1)
        if shift:
            wide = pltpu.roll(wide, shift, 1)
        gbuf[:, start : start + width] += wide
    ggrad[...] = gbuf[:HID].astype(BF16)
    ugrad[...] = gbuf[HID : 2 * HID].astype(BF16)
    dgrad[...] = gbuf[2 * HID :].astype(BF16)

    for copy in sent_q + sent_b:
        copy.wait_send()


def write_out(*refs):
    count = len(refs) // 2
    sems = refs[-1]
    copies = [
        pltpu.make_async_copy(refs[i], refs[count + i], sems.at[i]) for i in range(count)
    ]
    for copy in copies:
        copy.start()
    for copy in copies:
        copy.wait()


def per_device(tokens, cotangent, route_ids, gates, w_gate, w_up, w_down):
    rows, cols = tokens.shape
    hid, width = w_gate.shape
    share = width // NDP
    top = route_ids.shape[1]
    vmem = pl.BlockSpec(memory_space=pltpu.VMEM)
    hbm = pl.BlockSpec(memory_space=pl.ANY)
    chunk_of = (ROWS, LANES)
    real_of = (REAL, LANES)
    shapes = (
        jax.ShapeDtypeStruct((cols, rows), BF16),
        jax.ShapeDtypeStruct((cols, rows), BF16),
        jax.ShapeDtypeStruct((hid, share), BF16),
        jax.ShapeDtypeStruct((hid, share), BF16),
        jax.ShapeDtypeStruct((hid, share), BF16),
    )
    operands = (tokens.T, cotangent.T, route_ids.T, gates.T, w_gate, w_up, w_down)
    results = pl.pallas_call(
        kernel,
        out_shape=shapes,
        in_specs=[hbm] * 7,
        out_specs=[vmem] * 5,
        scratch_shapes=[
            pltpu.VMEM((cols, rows), BF16),
            pltpu.VMEM((cols, rows), BF16),
            pltpu.VMEM((top, rows), jnp.int32),
            pltpu.VMEM((top, rows), F32),
            pltpu.VMEM((3, hid, width), BF16),
            pltpu.VMEM((CHUNKS, LANES, LANES), BF16),
            pltpu.VMEM(chunk_of, BF16),
            pltpu.VMEM(chunk_of, BF16),
            pltpu.VMEM((CHUNKS,) + chunk_of, BF16),
            pltpu.VMEM(chunk_of, F32),
            pltpu.VMEM(chunk_of, F32),
            pltpu.VMEM(real_of, F32),
            pltpu.VMEM(chunk_of, BF16),
            pltpu.VMEM(chunk_of, BF16),
            pltpu.VMEM((NX * NZ, LANES, LANES), BF16),
            pltpu.VMEM((NDP, ROWS // 2, LANES), BF16),
            pltpu.VMEM((NDP - 1, NC * NZ) + chunk_of, BF16),
            pltpu.VMEM((NZ, NX) + chunk_of, F32),
            pltpu.VMEM((NZ,) + real_of, BF16),
            pltpu.VMEM((NZ, HALF, LANES), BF16),
            pltpu.VMEM((NZ, REAL - HALF, LANES), BF16),
            pltpu.VMEM((2,) + real_of, BF16),
            pltpu.VMEM((NZ,) + real_of, BF16),
            pltpu.VMEM((NZ,) + real_of, BF16),
            pltpu.VMEM((NZ,) + real_of, BF16),
            pltpu.VMEM((NZ,) + real_of, BF16),
            pltpu.VMEM((NZ - 1,) + real_of, BF16),
            pltpu.VMEM((NZ,) + real_of, BF16),
            pltpu.VMEM(real_of, F32),
            pltpu.VMEM(chunk_of, BF16),
            pltpu.VMEM(chunk_of, BF16),
            pltpu.VMEM((NZ * NC, 3 * hid, LANES), F32),
            pltpu.VMEM((3 * hid, share), F32),
            pltpu.SemaphoreType.DMA((N_SEMS,)),
            pltpu.SemaphoreType.REGULAR,
        ],
        compiler_params=pltpu.CompilerParams(
            collective_id=0, has_side_effects=True, vmem_limit_bytes=40 * 1024 * 1024
        ),
        name="experts",
    )(*[pltpu.with_memory_space_constraint(v, pltpu.HBM) for v in operands])
    results = pl.pallas_call(
        write_out,
        out_shape=shapes,
        in_specs=[vmem] * 5,
        out_specs=[hbm] * 5,
        scratch_shapes=[pltpu.SemaphoreType.DMA((5,))],
        compiler_params=pltpu.CompilerParams(vmem_limit_bytes=40 * 1024 * 1024),
        name="write_out",
    )(*results)
    return (results[0].T, results[1].T) + tuple(results[2:])


def solution(mesh):
    in_specs = (
        P(("dp", "expert"), "tensor"),
        P(("dp", "expert"), "tensor"),
        P(("dp", "expert"), None),
        P(("dp", "expert"), None),
        P(("expert", "tensor"), None),
        P(("expert", "tensor"), None),
        P(("expert", "tensor"), None),
    )
    out_specs = (
        P(("dp", "expert"), "tensor"),
        P(("dp", "expert"), "tensor"),
        P(("expert", "tensor"), "dp"),
        P(("expert", "tensor"), "dp"),
        P(("expert", "tensor"), "dp"),
    )
    return jax.shard_map(
        per_device, mesh=mesh, in_specs=in_specs, out_specs=out_specs, check_vma=False
    )
```

```python
import jax
import jax.numpy as jnp
from jax import lax
from jax.experimental import pallas as pl
from jax.experimental.pallas import tpu as pltpu
from jax.sharding import PartitionSpec as P

NX, NZ, NC = 4, 4, 2
NY = 8
NDP = 4
CHUNKS = NX * NZ * NC
BLK = 16
ROWS = NY * BLK
REAL = NY * 14
HALF = 64
QUART = ROWS // 4
LANES = 256
HID = 64
N_SEMS = 240
BF16 = jnp.bfloat16
F32 = jnp.float32


def wrap(value, size):
    return lax.rem(value, size)


def nt_dot(left, right):
    return lax.dot_general(left, right, (((1,), (1,)), ((), ())), preferred_element_type=F32)


def tn_dot(left, right):
    return lax.dot_general(left, right, (((0,), (0,)), ((), ())), preferred_element_type=F32)


def kernel(
    tok_in, cot_in, rid_in, gat_in, wg, wu, wd,
    mixed, tgrad, ggrad, ugrad, dgrad,
    tok, cot, rid, gat, wraw, wt, disp, landed, chunk, acc, acc_sib, acc_in, mine, theirs, wsib, compact,
    extra, kept, opp_out, opp_a, opp_b, opp_in, right_out, left_out,
    from_left, from_right, z_out, z_in, total, ret_out, ret, gpart, gbuf, sems, ready,
):
    dp = lax.axis_index("dp")
    y = lax.axis_index("expert")
    t = lax.axis_index("tensor")
    x = t // (NZ * NC)
    z = wrap(t // NC, NZ)
    c = wrap(t, NC)
    other = 1 - c
    xr, xl, xo = wrap(x + 1, NX), wrap(x + 3, NX), wrap(x + 2, NX)
    cols = tok.shape[0]
    count = [0]

    def take(n=1):
        base = count[0]
        count[0] += n
        assert count[0] <= N_SEMS
        return base

    def tensor_at(x_, z_, c_):
        return {"tensor": x_ * (NZ * NC) + z_ * NC + c_}

    def at(c_, x_, z_):
        return c_ * (NX * NZ) + x_ * NZ + z_

    upper_z = z // 2

    def z_at(k):
        return (z, 1 - z + 4 * upper_z, 2 - upper_z, 3 - 3 * upper_z)[k]

    sibling = tensor_at(x, z, other)
    right, left = tensor_at(xr, z, c), tensor_at(xl, z, c)

    def z_peer(k):
        return tensor_at(x, z_at(k), c)

    def y_peer(k):
        return {"expert": wrap(y + k, NY)}

    def dp_peer(k):
        return {"dp": wrap(dp + k, NDP)}

    barrier = pltpu.get_barrier_semaphore()
    partners = [y_peer(k) for k in range(1, NY)]
    partners += [z_peer(k) for k in range(1, NZ)]
    partners += [dp_peer(1), dp_peer(NDP - 1)]
    partners += [sibling, right, left, tensor_at(xo, z, c)]
    for where in partners:
        pl.semaphore_signal(barrier, inc=1, device_id=where, device_id_type=pl.DeviceIdType.MESH)

    def send(src, dst, recv, where):
        copy = pltpu.make_async_remote_copy(
            src_ref=src, dst_ref=dst, send_sem=sems.at[take()], recv_sem=sems.at[recv],
            device_id=where, device_id_type=pl.DeviceIdType.MESH,
        )
        copy.start()
        return copy

    def arrived(ref, sem):
        pltpu.make_async_copy(ref, ref, sems.at[sem]).wait()

    small = []
    for src, dst in ((rid_in, rid), (gat_in, gat), (tok_in, tok), (cot_in, cot)):
        small.append(pltpu.make_async_copy(src, dst, sems.at[take()]))
        small[-1].start()
    loads = []
    for i, ref in enumerate((wg, wu, wd)):
        loads.append(pltpu.make_async_copy(ref, wraw.at[i], sems.at[take()]))
        loads[-1].start()

    lane = lax.broadcasted_iota(jnp.int32, (ROWS, ROWS), 1)
    row = lax.broadcasted_iota(jnp.int32, (ROWS, ROWS), 0)
    label = row // BLK
    first = wrap(row // (BLK // 2), 2) == 0
    slot = wrap(row, BLK // 2)
    upto = jnp.where(row <= lane, 1.0, 0.0).astype(BF16)

    def packed(at_):
        place = wrap(at_, BLK // 2)
        half = wrap(at_ // (BLK // 2), 2)
        return jnp.where(place < 7, (REAL // 2) * half + 7 * (at_ // BLK) + place, -1)

    pack = jnp.where(row == packed(lane), 1.0, 0.0).astype(BF16)
    unpack = jnp.where(lane == packed(row), 1.0, 0.0).astype(BF16)
    disp[...] = jnp.zeros_like(disp)
    small[0].wait()
    small[1].wait()
    hits = jnp.zeros((ROWS, ROWS), F32)
    weight_of = jnp.zeros((ROWS, ROWS), F32)
    for k in range(rid.shape[0]):
        same = rid[k : k + 1, :] == label
        hits = hits + jnp.where(same, 1.0, 0.0)
        weight_of = weight_of + jnp.where(same, gat[k : k + 1, :], 0.0)
    places = jnp.dot(hits.astype(BF16), upto, preferred_element_type=F32) - 1.0
    pick = jnp.where((hits == 1.0) & (places == slot.astype(F32)), 1.0, 0.0)
    slot_gate = jnp.sum(pick * weight_of, axis=1, keepdims=True)
    pick_tok = jnp.where(first, pick, 0.0).astype(BF16)
    pick_cot = jnp.where(first, 0.0, pick).astype(BF16)
    small[2].wait()
    small[3].wait()
    rows_tok = nt_dot(pick_tok, tok[...])
    rows_cot = nt_dot(pick_cot, cot[...])
    disp[:, 0:cols] = (rows_tok + slot_gate * rows_cot).astype(BF16)

    pl.semaphore_wait(barrier, len(partners))
    pl.semaphore_signal(
        ready, inc=1, device_id=dp_peer(NDP - 1), device_id_type=pl.DeviceIdType.MESH
    )

    me = at(c, x, z)
    my_rows = pl.ds(pl.multiple_of(y * BLK, BLK), BLK)
    sent_y = []
    y_in = take(NY - 1)
    for k in range(1, NY):
        there = pl.ds(pl.multiple_of(wrap(y + k, NY) * BLK, BLK), BLK)
        sent_y.append(send(disp.at[there], landed.at[my_rows], y_in + k - 1, y_peer(k)))
    landed[my_rows, :] = disp[my_rows, :]
    chunk[:, REAL:, :] = jnp.zeros((CHUNKS, ROWS - REAL, LANES), BF16)

    for copy in loads:
        copy.wait()
    wt[:, :, LANES // 2 :] = jnp.zeros((CHUNKS, LANES, LANES // 2), BF16)
    wt[:, 3 * HID :, : LANES // 2] = jnp.zeros((CHUNKS, LANES - 3 * HID, LANES // 2), BF16)
    for tt in range(CHUNKS):
        g = at(tt % NC, tt // (NZ * NC), (tt // NC) % NZ)
        for i in range(3):
            wt[g, HID * i : HID * (i + 1), 0:cols] = wraw[i, :, cols * tt : cols * (tt + 1)]
    acc[...] = jnp.zeros_like(acc)
    acc_sib[...] = jnp.zeros_like(acc_sib)
    wsib[:, 3 * HID :, :] = jnp.zeros((NX * NZ, LANES - 3 * HID, LANES), BF16)
    w_sem = take()
    held = pl.ds(0, 3 * HID)
    give = pl.ds(pl.multiple_of(other * (NX * NZ), NX * NZ), NX * NZ)
    sent_w = [send(wt.at[give, held], wsib.at[:, held], w_sem, sibling)]

    for k in range(1, NY):
        from_y = pl.ds(pl.multiple_of(wrap(y + NY - k, NY) * BLK, BLK), BLK)
        arrived(landed.at[from_y], y_in + k - 1)
    chunk[me] = jnp.dot(pack, landed[...], preferred_element_type=F32).astype(BF16)

    def consume(x_, k):
        zk = z_at(k)
        g = at(c, x_, zk)
        value = chunk[g]
        acc[...] += nt_dot(value, wt[g])
        acc_sib[...] += nt_dot(value, wsib[x_ * NZ + zk])

    z_sem = take(NZ)
    left_sem, right_sem = take(NZ), take(NZ)
    oa_sem, ob_sem = take(NZ), take(NZ)
    sent_g = []
    sent_q = []
    opposite = tensor_at(xo, z, c)
    straight = (0, 3)
    bend = (0, 1, 2, 3)

    def real(g, start=0, size=REAL):
        return chunk.at[g, pl.ds(start, size)]

    def pass_on(ref, sem, where):
        sent_g.append(send(ref, ref, sem, where))

    def from_z(k):
        zk = z_at(k)
        g = at(c, x, zk)
        if k > 0:
            arrived(real(g), z_sem + zk)
        pass_on(real(g), left_sem + zk, right)
        pass_on(real(g), right_sem + zk, left)
        if k in straight:
            pass_on(real(g), oa_sem + zk, opposite)
        if k == 0:
            for j in range(1, NZ):
                pass_on(real(g), z_sem + z, z_peer(j))

    def from_x(k):
        zk = z_at(k)
        g = at(c, xl, zk)
        arrived(real(g), left_sem + zk)
        if k not in straight:
            pass_on(real(g, 0, HALF), oa_sem + zk, right)
        g = at(c, xr, zk)
        arrived(real(g), right_sem + zk)
        if k not in straight:
            pass_on(real(g, HALF, REAL - HALF), ob_sem + zk, left)

    def from_o(k):
        zk = z_at(k)
        g = at(c, xo, zk)
        if k in straight:
            arrived(real(g), oa_sem + zk)
        else:
            arrived(real(g, 0, HALF), oa_sem + zk)
            arrived(real(g, HALF, REAL - HALF), ob_sem + zk)

    quarter = pl.ds(pl.multiple_of(x * QUART, QUART), QUART)
    q_sem = take(NDP - 1)

    def across():
        pl.semaphore_wait(ready, 1)
        for k in range(1, NDP):
            src = chunk.at[at(c, wrap(dp + k, NDP), z), quarter]
            sent_q.append(send(src, extra.at[k - 1, c * NZ + z, quarter], q_sem + k - 1, dp_peer(k)))

    from_z(0)
    from_z(1)
    from_x(0)
    from_z(2)
    from_o(0)
    across()
    from_x(1)
    arrived(wsib.at[:, held], w_sem)
    consume(x, 0)
    consume(x, 1)
    from_z(3)
    consume(xl, 0)
    consume(xr, 0)
    consume(x, 2)
    from_x(2)
    consume(xo, 0)
    consume(xl, 1)
    consume(xr, 1)
    from_o(1)
    consume(x, 3)
    consume(xl, 2)
    consume(xr, 2)
    from_x(3)
    consume(xo, 1)
    from_o(2)
    consume(xl, 3)
    consume(xr, 3)
    consume(xo, 2)
    from_o(3)
    consume(xo, 3)

    acc_sem, slots_sem, theirs_sem = take(), take(), take()
    own_rows = pl.ds(0, REAL)
    sent_w.append(send(acc_sib.at[own_rows], acc_in, acc_sem, sibling))
    mine_at = pl.ds(pl.multiple_of(c * (NX * NZ) + dp * NZ, NZ), NZ)
    other_at = pl.ds(pl.multiple_of(other * (NX * NZ) + dp * NZ, NZ), NZ)
    slots = chunk.at[mine_at, own_rows]
    sent_w.append(send(slots, slots, slots_sem, sibling))
    arrived(acc_in, acc_sem)
    acc[:REAL] += acc_in[...]

    half_rows = REAL // 2
    fwd = acc[:half_rows, : 2 * HID]
    bwd = acc[half_rows:REAL, 2 * HID :]
    low = lax.broadcasted_iota(jnp.int32, (half_rows, 2 * HID), 1) < HID
    turned = pltpu.roll(fwd, HID, 1)
    pre = jnp.where(low, fwd, turned)
    upper = jnp.where(low, turned, fwd)
    back = bwd + pltpu.roll(bwd, HID, 1)
    sig = jax.nn.sigmoid(pre)
    act = pre * sig
    hidden = act * upper
    gate_delta = back * upper * sig * (1.0 + pre * (1.0 - sig))
    up_delta = back * act
    deltas = jnp.where(low, gate_delta, up_delta)
    hid = jnp.where(low, hidden, 0.0)
    zeros = jnp.zeros((half_rows, 2 * HID), F32)
    pad = jnp.zeros((ROWS // 2 - half_rows, LANES), F32)
    tail = jnp.zeros((ROWS - REAL, LANES), F32)
    top = jnp.concatenate([zeros, hid], axis=1)
    bottom = jnp.concatenate([deltas, zeros], axis=1)
    mine[...] = jnp.concatenate([top, bottom, tail], axis=0).astype(BF16)

    sent_w.append(send(mine, theirs, theirs_sem, sibling))
    compact[NDP - 1] = jnp.concatenate(
        [jnp.concatenate([deltas, hid], axis=1), pad], axis=0
    ).astype(BF16)
    m_sem = take(NDP - 1)
    sent_m = []
    for k in range(1, NDP):
        sent_m.append(send(compact.at[NDP - 1], compact.at[k - 1], m_sem + k - 1, dp_peer(k)))

    xa_sem, xb_sem = take(NZ), take(NZ)
    nl_sem, nr_sem = take(NZ), take(NZ)
    zr_sem = take(NZ)
    sent_r = []

    def stage_a(k):
        zk = z_at(NZ - 1 - k) if k < NZ - 1 else z
        ours, other_side = mine[...], theirs[...]

        def one(x_, carry):
            kept[k, x_] = jnp.dot(ours, wt[at(c, x_, zk)], preferred_element_type=F32) + jnp.dot(
                other_side, wsib[x_ * NZ + zk], preferred_element_type=F32
            )
            return carry

        lax.fori_loop(0, NX, one, 0)

    def pair(k, x_):
        return kept[k, x_, :REAL]

    def stage_b(k):
        opp_out[k] = pair(k, xo).astype(BF16)
        if k in bend:
            sent_r.append(send(opp_out.at[k], opp_in.at[k], xa_sem + k, opposite))
            return
        sent_r.append(send(opp_out.at[k, pl.ds(0, HALF)], opp_a.at[k], xa_sem + k, right))
        sent_r.append(send(opp_out.at[k, pl.ds(HALF, REAL - HALF)], opp_b.at[k], xb_sem + k, left))

    def stage_c(k):
        value = pair(k, xr)
        if k in bend:
            right_out[k] = value.astype(BF16)
        else:
            arrived(opp_a.at[k], xa_sem + k)
            right_out[k, :HALF] = (value[:HALF] + opp_a[k].astype(F32)).astype(BF16)
            right_out[k, HALF:] = value[HALF:].astype(BF16)
        sent_r.append(send(right_out.at[k], from_left.at[k], nl_sem + k, right))
        value = pair(k, xl)
        if k in bend:
            left_out[k] = value.astype(BF16)
        else:
            arrived(opp_b.at[k], xb_sem + k)
            left_out[k, :HALF] = value[:HALF].astype(BF16)
            left_out[k, HALF:] = (value[HALF:] + opp_b[k].astype(F32)).astype(BF16)
        sent_r.append(send(left_out.at[k], from_right.at[k], nr_sem + k, left))

    def stage_d(k):
        arrived(from_left.at[k], nl_sem + k)
        arrived(from_right.at[k], nr_sem + k)
        value = pair(k, x) + from_left[k].astype(F32) + from_right[k].astype(F32)
        if k in bend:
            arrived(opp_in.at[k], xa_sem + k)
            value = value + opp_in[k].astype(F32)
        if k < NZ - 1:
            z_out[k] = value.astype(BF16)
            sent_r.append(send(z_out.at[k], z_in.at[z], zr_sem + z, z_peer(NZ - 1 - k)))
        else:
            total[...] = value

    qz_sem = take(NZ)
    ql_sem, qr_sem, qa_sem, qb_sem = take(NZ), take(NZ), take(NZ), take(NZ)
    qs_sem = take(NZ)

    def part_rows(x_, start, size):
        return pl.ds(pl.multiple_of(x_ * QUART + start, BLK), size)

    def spread_1():
        for k in range(1, NDP):
            arrived(extra.at[k - 1, c * NZ + z, quarter], q_sem + k - 1)
        piece = extra.at[:, c * NZ + z, quarter]
        for k in range(1, NZ):
            sent_q.append(send(piece, piece, qz_sem + z, z_peer(k)))
        sent_q.append(send(piece, piece, ql_sem + 0, right))
        sent_q.append(send(piece, piece, qa_sem + 0, opposite))
        sent_q.append(send(piece, piece, qr_sem + 0, left))

    def spread_2(k):
        piece = extra.at[:, c * NZ + z_at(k), quarter]
        arrived(piece, qz_sem + z_at(k))
        sent_q.append(send(piece, piece, ql_sem + k, right))
        sent_q.append(send(piece, piece, qa_sem + k, opposite))
        sent_q.append(send(piece, piece, qr_sem + k, left))

    def spread_4(k):
        here = c * NZ + z_at(k)
        arrived(extra.at[:, here, part_rows(xl, 0, QUART)], ql_sem + k)
        arrived(extra.at[:, here, part_rows(xr, 0, QUART)], qr_sem + k)
        arrived(extra.at[:, here, part_rows(xo, 0, QUART)], qa_sem + k)
        piece = extra.at[:, here]
        sent_q.append(send(piece, piece, qs_sem + k, sibling))

    arrived(theirs, theirs_sem)
    stage_a(0)
    stage_b(0)
    stage_c(0)
    stage_a(1)
    stage_b(1)
    stage_c(1)
    stage_a(2)
    stage_b(2)
    stage_c(2)
    spread_1()
    stage_a(3)
    stage_b(3)
    stage_c(3)
    stage_d(0)
    spread_2(1)
    stage_d(1)
    spread_2(2)
    spread_2(3)
    stage_d(2)
    stage_d(3)

    value = total[...]
    for k in range(1, NZ):
        arrived(z_in.at[z_at(k)], zr_sem + z_at(k))
        value = value + z_in[z_at(k)].astype(F32)
    ret_out[...] = jnp.dot(
        unpack[:, :REAL], value.astype(BF16), preferred_element_type=F32
    ).astype(BF16)

    yr_sem = take(NY - 1)
    sent_b = []
    for k in range(1, NY):
        there = pl.ds(pl.multiple_of(wrap(y + k, NY) * BLK, BLK), BLK)
        sent_b.append(send(ret_out.at[there], ret.at[my_rows], yr_sem + k - 1, y_peer(k)))
    ret[my_rows, :] = ret_out[my_rows, :]
    spread_4(0)
    spread_4(1)
    spread_4(2)
    spread_4(3)

    for k in range(1, NDP):
        arrived(compact.at[k - 1], m_sem + k - 1)
    sides = []
    for k in range(NDP):
        both = compact[k, :half_rows].astype(F32)
        top = jnp.concatenate([both[:, : 2 * HID], zeros], axis=1)
        bottom = jnp.concatenate([zeros, both[:, 2 * HID :]], axis=1)
        side = jnp.concatenate([top, bottom, tail], axis=0)
        sides.append(jnp.transpose(side)[: 3 * HID].astype(BF16))
    def gradient(k):
        z_ = z_at(k)
        arrived(extra.at[:, other * NZ + z_], qs_sem + k)
        for c_ in range(NC):
            value = jnp.dot(sides[NDP - 1], chunk[at(c_, dp, z_)], preferred_element_type=F32)
            for j in range(1, NDP):
                value += jnp.dot(
                    sides[j - 1], extra[j - 1, c_ * NZ + z_], preferred_element_type=F32
                )
            gpart[z_ * NC + c_] = value

    for copy in sent_y + sent_g + sent_m + sent_r + sent_w:
        copy.wait_send()
    arrived(chunk.at[other_at, own_rows], slots_sem)
    gradient(0)
    gradient(1)
    gradient(2)

    gate_of = jnp.where(first, pick * weight_of, 0.0)
    high = gate_of.astype(BF16)
    low_part = (gate_of - high.astype(F32)).astype(BF16)
    back_to = jnp.concatenate([high, low_part, pick_cot], axis=1)
    for k in range(1, NY):
        from_y = pl.ds(pl.multiple_of(wrap(y + NY - k, NY) * BLK, BLK), BLK)
        arrived(ret.at[from_y], yr_sem + k - 1)
    got = ret[...]
    out = tn_dot(got, back_to)[:cols]
    mixed[...] = (out[:, :ROWS] + out[:, ROWS : 2 * ROWS]).astype(BF16)
    tgrad[...] = out[:, 2 * ROWS :].astype(BF16)

    gradient(3)
    gbuf[...] = jnp.zeros_like(gbuf)
    for i in range(NZ * NC):
        start = cols * i // 128 * 128
        shift = cols * i - start
        width = min(LANES + 128, gbuf.shape[1] - start)
        wide = gpart[i]
        if width > LANES:
            wide = jnp.concatenate([wide, jnp.zeros((3 * HID, width - LANES), F32)], axis=1)
        if shift:
            wide = pltpu.roll(wide, shift, 1)
        gbuf[:, start : start + width] += wide
    ggrad[...] = gbuf[:HID].astype(BF16)
    ugrad[...] = gbuf[HID : 2 * HID].astype(BF16)
    dgrad[...] = gbuf[2 * HID :].astype(BF16)

    for copy in sent_q + sent_b:
        copy.wait_send()


def write_out(*refs):
    count = len(refs) // 2
    sems = refs[-1]
    copies = [
        pltpu.make_async_copy(refs[i], refs[count + i], sems.at[i]) for i in range(count)
    ]
    for copy in copies:
        copy.start()
    for copy in copies:
        copy.wait()


def per_device(tokens, cotangent, route_ids, gates, w_gate, w_up, w_down):
    rows, cols = tokens.shape
    hid, width = w_gate.shape
    share = width // NDP
    top = route_ids.shape[1]
    vmem = pl.BlockSpec(memory_space=pltpu.VMEM)
    hbm = pl.BlockSpec(memory_space=pl.ANY)
    chunk_of = (ROWS, LANES)
    real_of = (REAL, LANES)
    shapes = (
        jax.ShapeDtypeStruct((cols, rows), BF16),
        jax.ShapeDtypeStruct((cols, rows), BF16),
        jax.ShapeDtypeStruct((hid, share), BF16),
        jax.ShapeDtypeStruct((hid, share), BF16),
        jax.ShapeDtypeStruct((hid, share), BF16),
    )
    operands = (tokens.T, cotangent.T, route_ids.T, gates.T, w_gate, w_up, w_down)
    results = pl.pallas_call(
        kernel,
        out_shape=shapes,
        in_specs=[hbm] * 7,
        out_specs=[vmem] * 5,
        scratch_shapes=[
            pltpu.VMEM((cols, rows), BF16),
            pltpu.VMEM((cols, rows), BF16),
            pltpu.VMEM((top, rows), jnp.int32),
            pltpu.VMEM((top, rows), F32),
            pltpu.VMEM((3, hid, width), BF16),
            pltpu.VMEM((CHUNKS, LANES, LANES), BF16),
            pltpu.VMEM(chunk_of, BF16),
            pltpu.VMEM(chunk_of, BF16),
            pltpu.VMEM((CHUNKS,) + chunk_of, BF16),
            pltpu.VMEM(chunk_of, F32),
            pltpu.VMEM(chunk_of, F32),
            pltpu.VMEM(real_of, F32),
            pltpu.VMEM(chunk_of, BF16),
            pltpu.VMEM(chunk_of, BF16),
            pltpu.VMEM((NX * NZ, LANES, LANES), BF16),
            pltpu.VMEM((NDP, ROWS // 2, LANES), BF16),
            pltpu.VMEM((NDP - 1, NC * NZ) + chunk_of, BF16),
            pltpu.VMEM((NZ, NX) + chunk_of, F32),
            pltpu.VMEM((NZ,) + real_of, BF16),
            pltpu.VMEM((NZ, HALF, LANES), BF16),
            pltpu.VMEM((NZ, REAL - HALF, LANES), BF16),
            pltpu.VMEM((NZ,) + real_of, BF16),
            pltpu.VMEM((NZ,) + real_of, BF16),
            pltpu.VMEM((NZ,) + real_of, BF16),
            pltpu.VMEM((NZ,) + real_of, BF16),
            pltpu.VMEM((NZ,) + real_of, BF16),
            pltpu.VMEM((NZ - 1,) + real_of, BF16),
            pltpu.VMEM((NZ,) + real_of, BF16),
            pltpu.VMEM(real_of, F32),
            pltpu.VMEM(chunk_of, BF16),
            pltpu.VMEM(chunk_of, BF16),
            pltpu.VMEM((NZ * NC, 3 * hid, LANES), F32),
            pltpu.VMEM((3 * hid, share), F32),
            pltpu.SemaphoreType.DMA((N_SEMS,)),
            pltpu.SemaphoreType.REGULAR,
        ],
        compiler_params=pltpu.CompilerParams(
            collective_id=0, has_side_effects=True, vmem_limit_bytes=40 * 1024 * 1024
        ),
        name="experts",
    )(*[pltpu.with_memory_space_constraint(v, pltpu.HBM) for v in operands])
    results = pl.pallas_call(
        write_out,
        out_shape=shapes,
        in_specs=[vmem] * 5,
        out_specs=[hbm] * 5,
        scratch_shapes=[pltpu.SemaphoreType.DMA((5,))],
        compiler_params=pltpu.CompilerParams(vmem_limit_bytes=40 * 1024 * 1024),
        name="write_out",
    )(*results)
    return (results[0].T, results[1].T) + tuple(results[2:])


def solution(mesh):
    in_specs = (
        P(("dp", "expert"), "tensor"),
        P(("dp", "expert"), "tensor"),
        P(("dp", "expert"), None),
        P(("dp", "expert"), None),
        P(("expert", "tensor"), None),
        P(("expert", "tensor"), None),
        P(("expert", "tensor"), None),
    )
    out_specs = (
        P(("dp", "expert"), "tensor"),
        P(("dp", "expert"), "tensor"),
        P(("expert", "tensor"), "dp"),
        P(("expert", "tensor"), "dp"),
        P(("expert", "tensor"), "dp"),
    )
    return jax.shard_map(
        per_device, mesh=mesh, in_specs=in_specs, out_specs=out_specs, check_vma=False
    )
```

```python
import jax
import jax.numpy as jnp
from jax import lax
from jax.experimental import pallas as pl
from jax.experimental.pallas import tpu as pltpu
from jax.sharding import PartitionSpec as P

NX, NZ, NC = 4, 4, 2
NY = 8
NDP = 4
CHUNKS = NX * NZ * NC
BLK = 16
ROWS = NY * BLK
REAL = NY * 14
HALF = 64
QUART = ROWS // 4
LANES = 256
HID = 64
N_SEMS = 240
BF16 = jnp.bfloat16
F32 = jnp.float32


def wrap(value, size):
    return lax.rem(value, size)


def nt_dot(left, right):
    return lax.dot_general(left, right, (((1,), (1,)), ((), ())), preferred_element_type=F32)


def tn_dot(left, right):
    return lax.dot_general(left, right, (((0,), (0,)), ((), ())), preferred_element_type=F32)


def kernel(
    tok_in, cot_in, rid_in, gat_in, wg, wu, wd,
    mixed, tgrad, ggrad, ugrad, dgrad,
    tok, cot, rid, gat, wraw, wt, disp, landed, chunk, acc, acc_sib, acc_in, mine, theirs, wsib, compact,
    extra, kept, opp_out, opp_a, opp_b, opp_in, right_out, left_out,
    from_left, from_right, z_out, z_in, total, ret_out, ret, gpart, gbuf, sems, ready,
):
    dp = lax.axis_index("dp")
    y = lax.axis_index("expert")
    t = lax.axis_index("tensor")
    x = t // (NZ * NC)
    z = wrap(t // NC, NZ)
    c = wrap(t, NC)
    other = 1 - c
    xr, xl, xo = wrap(x + 1, NX), wrap(x + 3, NX), wrap(x + 2, NX)
    cols = tok.shape[0]
    count = [0]

    def take(n=1):
        base = count[0]
        count[0] += n
        assert count[0] <= N_SEMS
        return base

    def tensor_at(x_, z_, c_):
        return {"tensor": x_ * (NZ * NC) + z_ * NC + c_}

    def at(c_, x_, z_):
        return c_ * (NX * NZ) + x_ * NZ + z_

    upper_z = z // 2

    def z_at(k):
        return (z, 1 - z + 4 * upper_z, 2 - upper_z, 3 - 3 * upper_z)[k]

    sibling = tensor_at(x, z, other)
    right, left = tensor_at(xr, z, c), tensor_at(xl, z, c)

    def z_peer(k):
        return tensor_at(x, z_at(k), c)

    def y_peer(k):
        return {"expert": wrap(y + k, NY)}

    def dp_peer(k):
        return {"dp": wrap(dp + k, NDP)}

    barrier = pltpu.get_barrier_semaphore()
    partners = [y_peer(k) for k in range(1, NY)]
    partners += [z_peer(k) for k in range(1, NZ)]
    partners += [dp_peer(1), dp_peer(NDP - 1)]
    partners += [sibling, right, left, tensor_at(xo, z, c)]
    for where in partners:
        pl.semaphore_signal(barrier, inc=1, device_id=where, device_id_type=pl.DeviceIdType.MESH)

    def send(src, dst, recv, where):
        copy = pltpu.make_async_remote_copy(
            src_ref=src, dst_ref=dst, send_sem=sems.at[take()], recv_sem=sems.at[recv],
            device_id=where, device_id_type=pl.DeviceIdType.MESH,
        )
        copy.start()
        return copy

    def arrived(ref, sem):
        pltpu.make_async_copy(ref, ref, sems.at[sem]).wait()

    small = []
    for src, dst in ((rid_in, rid), (gat_in, gat), (tok_in, tok), (cot_in, cot)):
        small.append(pltpu.make_async_copy(src, dst, sems.at[take()]))
        small[-1].start()
    loads = []
    for i, ref in enumerate((wg, wu, wd)):
        loads.append(pltpu.make_async_copy(ref, wraw.at[i], sems.at[take()]))
        loads[-1].start()

    lane = lax.broadcasted_iota(jnp.int32, (ROWS, ROWS), 1)
    row = lax.broadcasted_iota(jnp.int32, (ROWS, ROWS), 0)
    label = row // BLK
    first = wrap(row // (BLK // 2), 2) == 0
    slot = wrap(row, BLK // 2)
    upto = jnp.where(row <= lane, 1.0, 0.0).astype(BF16)

    def packed(at_):
        place = wrap(at_, BLK // 2)
        half = wrap(at_ // (BLK // 2), 2)
        return jnp.where(place < 7, (REAL // 2) * half + 7 * (at_ // BLK) + place, -1)

    pack = jnp.where(row == packed(lane), 1.0, 0.0).astype(BF16)
    unpack = jnp.where(lane == packed(row), 1.0, 0.0).astype(BF16)
    disp[...] = jnp.zeros_like(disp)
    small[0].wait()
    small[1].wait()
    hits = jnp.zeros((ROWS, ROWS), F32)
    weight_of = jnp.zeros((ROWS, ROWS), F32)
    for k in range(rid.shape[0]):
        same = rid[k : k + 1, :] == label
        hits = hits + jnp.where(same, 1.0, 0.0)
        weight_of = weight_of + jnp.where(same, gat[k : k + 1, :], 0.0)
    places = jnp.dot(hits.astype(BF16), upto, preferred_element_type=F32) - 1.0
    pick = jnp.where((hits == 1.0) & (places == slot.astype(F32)), 1.0, 0.0)
    slot_gate = jnp.sum(pick * weight_of, axis=1, keepdims=True)
    pick_tok = jnp.where(first, pick, 0.0).astype(BF16)
    pick_cot = jnp.where(first, 0.0, pick).astype(BF16)
    small[2].wait()
    small[3].wait()
    rows_tok = nt_dot(pick_tok, tok[...])
    rows_cot = nt_dot(pick_cot, cot[...])
    disp[:, 0:cols] = (rows_tok + slot_gate * rows_cot).astype(BF16)

    pl.semaphore_wait(barrier, len(partners))
    pl.semaphore_signal(
        ready, inc=1, device_id=dp_peer(NDP - 1), device_id_type=pl.DeviceIdType.MESH
    )

    me = at(c, x, z)
    my_rows = pl.ds(pl.multiple_of(y * BLK, BLK), BLK)
    sent_y = []
    y_in = take(NY - 1)
    for k in range(1, NY):
        there = pl.ds(pl.multiple_of(wrap(y + k, NY) * BLK, BLK), BLK)
        sent_y.append(send(disp.at[there], landed.at[my_rows], y_in + k - 1, y_peer(k)))
    landed[my_rows, :] = disp[my_rows, :]
    chunk[:, REAL:, :] = jnp.zeros((CHUNKS, ROWS - REAL, LANES), BF16)

    for copy in loads:
        copy.wait()
    wt[:, :, LANES // 2 :] = jnp.zeros((CHUNKS, LANES, LANES // 2), BF16)
    wt[:, 3 * HID :, : LANES // 2] = jnp.zeros((CHUNKS, LANES - 3 * HID, LANES // 2), BF16)
    for tt in range(CHUNKS):
        g = at(tt % NC, tt // (NZ * NC), (tt // NC) % NZ)
        for i in range(3):
            wt[g, HID * i : HID * (i + 1), 0:cols] = wraw[i, :, cols * tt : cols * (tt + 1)]
    acc[...] = jnp.zeros_like(acc)
    acc_sib[...] = jnp.zeros_like(acc_sib)
    wsib[:, 3 * HID :, :] = jnp.zeros((NX * NZ, LANES - 3 * HID, LANES), BF16)
    w_sem = take()
    held = pl.ds(0, 3 * HID)
    give = pl.ds(pl.multiple_of(other * (NX * NZ), NX * NZ), NX * NZ)
    sent_w = [send(wt.at[give, held], wsib.at[:, held], w_sem, sibling)]

    for k in range(1, NY):
        from_y = pl.ds(pl.multiple_of(wrap(y + NY - k, NY) * BLK, BLK), BLK)
        arrived(landed.at[from_y], y_in + k - 1)
    chunk[me] = jnp.dot(pack, landed[...], preferred_element_type=F32).astype(BF16)

    def consume(x_, k):
        zk = z_at(k)
        g = at(c, x_, zk)
        value = chunk[g]
        acc[...] += nt_dot(value, wt[g])
        acc_sib[...] += nt_dot(value, wsib[x_ * NZ + zk])

    z_sem = take(NZ)
    left_sem, right_sem = take(NZ), take(NZ)
    oa_sem, ob_sem = take(NZ), take(NZ)
    sent_g = []
    sent_q = []
    opposite = tensor_at(xo, z, c)
    straight = (0, 3)
    bend = (0, 3)

    def real(g, start=0, size=REAL):
        return chunk.at[g, pl.ds(start, size)]

    def pass_on(ref, sem, where):
        sent_g.append(send(ref, ref, sem, where))

    def from_z(k):
        zk = z_at(k)
        g = at(c, x, zk)
        if k > 0:
            arrived(real(g), z_sem + zk)
        pass_on(real(g), left_sem + zk, right)
        pass_on(real(g), right_sem + zk, left)
        if k in straight:
            pass_on(real(g), oa_sem + zk, opposite)
        if k == 0:
            for j in range(1, NZ):
                pass_on(real(g), z_sem + z, z_peer(j))

    def from_x(k):
        zk = z_at(k)
        g = at(c, xl, zk)
        arrived(real(g), left_sem + zk)
        if k not in straight:
            pass_on(real(g, 0, HALF), oa_sem + zk, right)
        g = at(c, xr, zk)
        arrived(real(g), right_sem + zk)
        if k not in straight:
            pass_on(real(g, HALF, REAL - HALF), ob_sem + zk, left)

    def from_o(k):
        zk = z_at(k)
        g = at(c, xo, zk)
        if k in straight:
            arrived(real(g), oa_sem + zk)
        else:
            arrived(real(g, 0, HALF), oa_sem + zk)
            arrived(real(g, HALF, REAL - HALF), ob_sem + zk)

    quarter = pl.ds(pl.multiple_of(x * QUART, QUART), QUART)
    q_sem = take(NDP - 1)

    def across():
        pl.semaphore_wait(ready, 1)
        for k in range(1, NDP):
            src = chunk.at[at(c, wrap(dp + k, NDP), z), quarter]
            sent_q.append(send(src, extra.at[k - 1, c * NZ + z, quarter], q_sem + k - 1, dp_peer(k)))

    from_z(0)
    from_z(1)
    from_x(0)
    from_z(2)
    from_o(0)
    across()
    from_x(1)
    arrived(wsib.at[:, held], w_sem)
    consume(x, 0)
    consume(x, 1)
    from_z(3)
    consume(xl, 0)
    consume(xr, 0)
    consume(x, 2)
    from_x(2)
    consume(xo, 0)
    consume(xl, 1)
    consume(xr, 1)
    from_o(1)
    consume(x, 3)
    consume(xl, 2)
    consume(xr, 2)
    from_x(3)
    consume(xo, 1)
    from_o(2)
    consume(xl, 3)
    consume(xr, 3)
    consume(xo, 2)
    from_o(3)
    consume(xo, 3)

    acc_sem, slots_sem, theirs_sem = take(), take(), take()
    own_rows = pl.ds(0, REAL)
    sent_w.append(send(acc_sib.at[own_rows], acc_in, acc_sem, sibling))
    mine_at = pl.ds(pl.multiple_of(c * (NX * NZ) + dp * NZ, NZ), NZ)
    other_at = pl.ds(pl.multiple_of(other * (NX * NZ) + dp * NZ, NZ), NZ)
    slots = chunk.at[mine_at, own_rows]
    sent_w.append(send(slots, slots, slots_sem, sibling))
    arrived(acc_in, acc_sem)
    acc[:REAL] += acc_in[...]

    half_rows = REAL // 2
    fwd = acc[:half_rows, : 2 * HID]
    bwd = acc[half_rows:REAL, 2 * HID :]
    low = lax.broadcasted_iota(jnp.int32, (half_rows, 2 * HID), 1) < HID
    turned = pltpu.roll(fwd, HID, 1)
    pre = jnp.where(low, fwd, turned)
    upper = jnp.where(low, turned, fwd)
    back = bwd + pltpu.roll(bwd, HID, 1)
    sig = jax.nn.sigmoid(pre)
    act = pre * sig
    hidden = act * upper
    gate_delta = back * upper * sig * (1.0 + pre * (1.0 - sig))
    up_delta = back * act
    deltas = jnp.where(low, gate_delta, up_delta)
    hid = jnp.where(low, hidden, 0.0)
    zeros = jnp.zeros((half_rows, 2 * HID), F32)
    pad = jnp.zeros((ROWS // 2 - half_rows, LANES), F32)
    tail = jnp.zeros((ROWS - REAL, LANES), F32)
    top = jnp.concatenate([zeros, hid], axis=1)
    bottom = jnp.concatenate([deltas, zeros], axis=1)
    mine[...] = jnp.concatenate([top, bottom, tail], axis=0).astype(BF16)

    sent_w.append(send(mine, theirs, theirs_sem, sibling))
    wide_hid = jnp.concatenate([hid, jnp.zeros((ROWS // 2 - half_rows, 2 * HID), F32)], axis=0)
    folded = wide_hid[: ROWS // 4] + pltpu.roll(wide_hid[ROWS // 4 :], HID, 1)
    gap = jnp.zeros((ROWS // 2 - half_rows, 2 * HID), F32)
    compact[NDP - 1] = jnp.concatenate([deltas, gap, folded], axis=0).astype(BF16)
    m_sem = take(NDP - 1)
    sent_m = []
    for k in range(1, NDP):
        sent_m.append(send(compact.at[NDP - 1], compact.at[k - 1], m_sem + k - 1, dp_peer(k)))

    xa_sem, xb_sem = take(NZ), take(NZ)
    nl_sem, nr_sem = take(NZ), take(NZ)
    zr_sem = take(NZ)
    sent_r = []

    def stage_a(k):
        zk = z_at(NZ - 1 - k) if k < NZ - 1 else z
        ours, other_side = mine[...], theirs[...]

        def one(x_, carry):
            kept[k, x_] = jnp.dot(ours, wt[at(c, x_, zk)], preferred_element_type=F32) + jnp.dot(
                other_side, wsib[x_ * NZ + zk], preferred_element_type=F32
            )
            return carry

        lax.fori_loop(0, NX, one, 0)

    def pair(k, x_):
        return kept[k, x_, :REAL]

    def stage_b(k):
        opp_out[k] = pair(k, xo).astype(BF16)
        if k in bend:
            sent_r.append(send(opp_out.at[k], opp_in.at[k], xa_sem + k, opposite))
            return
        sent_r.append(send(opp_out.at[k, pl.ds(0, HALF)], opp_a.at[k], xa_sem + k, right))
        sent_r.append(send(opp_out.at[k, pl.ds(HALF, REAL - HALF)], opp_b.at[k], xb_sem + k, left))

    def stage_c(k):
        value = pair(k, xr)
        if k in bend:
            right_out[k] = value.astype(BF16)
        else:
            arrived(opp_a.at[k], xa_sem + k)
            right_out[k, :HALF] = (value[:HALF] + opp_a[k].astype(F32)).astype(BF16)
            right_out[k, HALF:] = value[HALF:].astype(BF16)
        sent_r.append(send(right_out.at[k], from_left.at[k], nl_sem + k, right))
        value = pair(k, xl)
        if k in bend:
            left_out[k] = value.astype(BF16)
        else:
            arrived(opp_b.at[k], xb_sem + k)
            left_out[k, :HALF] = value[:HALF].astype(BF16)
            left_out[k, HALF:] = (value[HALF:] + opp_b[k].astype(F32)).astype(BF16)
        sent_r.append(send(left_out.at[k], from_right.at[k], nr_sem + k, left))

    def stage_d(k):
        arrived(from_left.at[k], nl_sem + k)
        arrived(from_right.at[k], nr_sem + k)
        value = pair(k, x) + from_left[k].astype(F32) + from_right[k].astype(F32)
        if k in bend:
            arrived(opp_in.at[k], xa_sem + k)
            value = value + opp_in[k].astype(F32)
        if k < NZ - 1:
            z_out[k] = value.astype(BF16)
            sent_r.append(send(z_out.at[k], z_in.at[z], zr_sem + z, z_peer(NZ - 1 - k)))
        else:
            total[...] = value

    qz_sem = take(NZ)
    ql_sem, qr_sem, qa_sem, qb_sem = take(NZ), take(NZ), take(NZ), take(NZ)
    qs_sem = take(NZ)

    def part_rows(x_, start, size):
        return pl.ds(pl.multiple_of(x_ * QUART + start, BLK), size)

    def spread_1():
        for k in range(1, NDP):
            arrived(extra.at[k - 1, c * NZ + z, quarter], q_sem + k - 1)
        piece = extra.at[:, c * NZ + z, quarter]
        for k in range(1, NZ):
            sent_q.append(send(piece, piece, qz_sem + z, z_peer(k)))
        sent_q.append(send(piece, piece, ql_sem + 0, right))
        sent_q.append(send(piece, piece, qr_sem + 0, left))

    def spread_2(k):
        piece = extra.at[:, c * NZ + z_at(k), quarter]
        arrived(piece, qz_sem + z_at(k))
        sent_q.append(send(piece, piece, ql_sem + k, right))
        sent_q.append(send(piece, piece, qr_sem + k, left))

    def spread_3(k):
        here = c * NZ + z_at(k)
        arrived(extra.at[:, here, part_rows(xl, 0, QUART)], ql_sem + k)
        piece = extra.at[:, here, part_rows(xl, 0, QUART // 2)]
        sent_q.append(send(piece, piece, qa_sem + k, right))
        arrived(extra.at[:, here, part_rows(xr, 0, QUART)], qr_sem + k)
        piece = extra.at[:, here, part_rows(xr, QUART // 2, QUART // 2)]
        sent_q.append(send(piece, piece, qb_sem + k, left))

    def spread_4(k):
        here = c * NZ + z_at(k)
        arrived(extra.at[:, here, part_rows(xo, 0, QUART // 2)], qa_sem + k)
        arrived(extra.at[:, here, part_rows(xo, QUART // 2, QUART // 2)], qb_sem + k)
        piece = extra.at[:, here]
        sent_q.append(send(piece, piece, qs_sem + k, sibling))

    arrived(theirs, theirs_sem)
    stage_a(0)
    stage_b(0)
    stage_c(0)
    stage_a(1)
    stage_b(1)
    stage_a(2)
    stage_b(2)
    spread_1()
    stage_c(1)
    stage_a(3)
    stage_d(0)
    stage_c(2)
    stage_d(1)
    spread_2(1)
    stage_b(3)
    stage_c(3)
    spread_3(0)
    spread_2(2)
    spread_2(3)
    stage_d(2)
    stage_d(3)

    value = total[...]
    for k in range(1, NZ):
        arrived(z_in.at[z_at(k)], zr_sem + z_at(k))
        value = value + z_in[z_at(k)].astype(F32)
    ret_out[...] = jnp.dot(
        unpack[:, :REAL], value.astype(BF16), preferred_element_type=F32
    ).astype(BF16)

    yr_sem = take(NY - 1)
    sent_b = []
    for k in range(1, NY):
        there = pl.ds(pl.multiple_of(wrap(y + k, NY) * BLK, BLK), BLK)
        sent_b.append(send(ret_out.at[there], ret.at[my_rows], yr_sem + k - 1, y_peer(k)))
    ret[my_rows, :] = ret_out[my_rows, :]
    spread_4(0)
    for k in range(1, NZ):
        spread_3(k)
    for k in range(1, NZ):
        spread_4(k)

    for k in range(1, NDP):
        arrived(compact.at[k - 1], m_sem + k - 1)
    sides = []
    for k in range(NDP):
        both = compact[k].astype(F32)
        folded = both[ROWS // 2 :]
        unfolded = jnp.concatenate([folded, pltpu.roll(folded, HID, 1)], axis=0)[:half_rows]
        top = jnp.concatenate([both[:half_rows], zeros], axis=1)
        bottom = jnp.concatenate([zeros, jnp.where(low, unfolded, 0.0)], axis=1)
        side = jnp.concatenate([top, bottom, tail], axis=0)
        sides.append(jnp.transpose(side)[: 3 * HID].astype(BF16))
    def gradient(k):
        z_ = z_at(k)
        arrived(extra.at[:, other * NZ + z_], qs_sem + k)
        for c_ in range(NC):
            value = jnp.dot(sides[NDP - 1], chunk[at(c_, dp, z_)], preferred_element_type=F32)
            for j in range(1, NDP):
                value += jnp.dot(
                    sides[j - 1], extra[j - 1, c_ * NZ + z_], preferred_element_type=F32
                )
            gpart[z_ * NC + c_] = value

    for copy in sent_y + sent_g + sent_m + sent_r + sent_w:
        copy.wait_send()
    arrived(chunk.at[other_at, own_rows], slots_sem)
    gradient(0)
    gradient(1)
    gradient(2)

    gate_of = jnp.where(first, pick * weight_of, 0.0)
    high = gate_of.astype(BF16)
    low_part = (gate_of - high.astype(F32)).astype(BF16)
    back_to = jnp.concatenate([high, low_part, pick_cot], axis=1)
    for k in range(1, NY):
        from_y = pl.ds(pl.multiple_of(wrap(y + NY - k, NY) * BLK, BLK), BLK)
        arrived(ret.at[from_y], yr_sem + k - 1)
    got = ret[...]
    out = tn_dot(got, back_to)[:cols]
    mixed[...] = (out[:, :ROWS] + out[:, ROWS : 2 * ROWS]).astype(BF16)
    tgrad[...] = out[:, 2 * ROWS :].astype(BF16)

    gradient(3)
    gbuf[...] = jnp.zeros_like(gbuf)
    for i in range(NZ * NC):
        start = cols * i // 128 * 128
        shift = cols * i - start
        width = min(LANES + 128, gbuf.shape[1] - start)
        wide = gpart[i]
        if width > LANES:
            wide = jnp.concatenate([wide, jnp.zeros((3 * HID, width - LANES), F32)], axis=1)
        if shift:
            wide = pltpu.roll(wide, shift, 1)
        gbuf[:, start : start + width] += wide
    ggrad[...] = gbuf[:HID].astype(BF16)
    ugrad[...] = gbuf[HID : 2 * HID].astype(BF16)
    dgrad[...] = gbuf[2 * HID :].astype(BF16)

    for copy in sent_q + sent_b:
        copy.wait_send()


def write_out(*refs):
    count = len(refs) // 2
    sems = refs[-1]
    copies = [
        pltpu.make_async_copy(refs[i], refs[count + i], sems.at[i]) for i in range(count)
    ]
    for copy in copies:
        copy.start()
    for copy in copies:
        copy.wait()


def per_device(tokens, cotangent, route_ids, gates, w_gate, w_up, w_down):
    rows, cols = tokens.shape
    hid, width = w_gate.shape
    share = width // NDP
    top = route_ids.shape[1]
    vmem = pl.BlockSpec(memory_space=pltpu.VMEM)
    hbm = pl.BlockSpec(memory_space=pl.ANY)
    chunk_of = (ROWS, LANES)
    real_of = (REAL, LANES)
    shapes = (
        jax.ShapeDtypeStruct((cols, rows), BF16),
        jax.ShapeDtypeStruct((cols, rows), BF16),
        jax.ShapeDtypeStruct((hid, share), BF16),
        jax.ShapeDtypeStruct((hid, share), BF16),
        jax.ShapeDtypeStruct((hid, share), BF16),
    )
    operands = (tokens.T, cotangent.T, route_ids.T, gates.T, w_gate, w_up, w_down)
    results = pl.pallas_call(
        kernel,
        out_shape=shapes,
        in_specs=[hbm] * 7,
        out_specs=[vmem] * 5,
        scratch_shapes=[
            pltpu.VMEM((cols, rows), BF16),
            pltpu.VMEM((cols, rows), BF16),
            pltpu.VMEM((top, rows), jnp.int32),
            pltpu.VMEM((top, rows), F32),
            pltpu.VMEM((3, hid, width), BF16),
            pltpu.VMEM((CHUNKS, LANES, LANES), BF16),
            pltpu.VMEM(chunk_of, BF16),
            pltpu.VMEM(chunk_of, BF16),
            pltpu.VMEM((CHUNKS,) + chunk_of, BF16),
            pltpu.VMEM(chunk_of, F32),
            pltpu.VMEM(chunk_of, F32),
            pltpu.VMEM(real_of, F32),
            pltpu.VMEM(chunk_of, BF16),
            pltpu.VMEM(chunk_of, BF16),
            pltpu.VMEM((NX * NZ, LANES, LANES), BF16),
            pltpu.VMEM((NDP, 3 * ROWS // 4, LANES // 2), BF16),
            pltpu.VMEM((NDP - 1, NC * NZ) + chunk_of, BF16),
            pltpu.VMEM((NZ, NX) + chunk_of, F32),
            pltpu.VMEM((NZ,) + real_of, BF16),
            pltpu.VMEM((NZ, HALF, LANES), BF16),
            pltpu.VMEM((NZ, REAL - HALF, LANES), BF16),
            pltpu.VMEM((NZ,) + real_of, BF16),
            pltpu.VMEM((NZ,) + real_of, BF16),
            pltpu.VMEM((NZ,) + real_of, BF16),
            pltpu.VMEM((NZ,) + real_of, BF16),
            pltpu.VMEM((NZ,) + real_of, BF16),
            pltpu.VMEM((NZ - 1,) + real_of, BF16),
            pltpu.VMEM((NZ,) + real_of, BF16),
            pltpu.VMEM(real_of, F32),
            pltpu.VMEM(chunk_of, BF16),
            pltpu.VMEM(chunk_of, BF16),
            pltpu.VMEM((NZ * NC, 3 * hid, LANES), F32),
            pltpu.VMEM((3 * hid, share), F32),
            pltpu.SemaphoreType.DMA((N_SEMS,)),
            pltpu.SemaphoreType.REGULAR,
        ],
        compiler_params=pltpu.CompilerParams(
            collective_id=0, has_side_effects=True, vmem_limit_bytes=40 * 1024 * 1024
        ),
        name="experts",
    )(*[pltpu.with_memory_space_constraint(v, pltpu.HBM) for v in operands])
    results = pl.pallas_call(
        write_out,
        out_shape=shapes,
        in_specs=[vmem] * 5,
        out_specs=[hbm] * 5,
        scratch_shapes=[pltpu.SemaphoreType.DMA((5,))],
        compiler_params=pltpu.CompilerParams(vmem_limit_bytes=40 * 1024 * 1024),
        name="write_out",
    )(*results)
    return (results[0].T, results[1].T) + tuple(results[2:])


def solution(mesh):
    in_specs = (
        P(("dp", "expert"), "tensor"),
        P(("dp", "expert"), "tensor"),
        P(("dp", "expert"), None),
        P(("dp", "expert"), None),
        P(("expert", "tensor"), None),
        P(("expert", "tensor"), None),
        P(("expert", "tensor"), None),
    )
    out_specs = (
        P(("dp", "expert"), "tensor"),
        P(("dp", "expert"), "tensor"),
        P(("expert", "tensor"), "dp"),
        P(("expert", "tensor"), "dp"),
        P(("expert", "tensor"), "dp"),
    )
    return jax.shard_map(
        per_device, mesh=mesh, in_specs=in_specs, out_specs=out_specs, check_vma=False
    )
```
